256 devices in a mesh: group: 32 (over y, z_hi, core), tensor: 4 (over x), dp: 2 (over z_lo).
Axes of the slice: x: 4, y: 4, z: 8 (z_hi: 4, z_lo: 2; z = z_hi * 2 + z_lo), core: 2. Of those that a mesh axis runs over, the one named last changes fastest.
Arguments:
- queries: bfloat16 [2, 32, 256, 5120], P('dp', 'group', 'tensor'), may hold values from -32 to 32
- suffix_keys: bfloat16 [2, 32, 256, 1024], P('dp', 'group', 'tensor'), may hold values from -6 to 6
- suffix_values: bfloat16 [2, 32, 256, 1024], P('dp', 'group', 'tensor'), may hold values from -6 to 6
- d_out: bfloat16 [2, 32, 256, 5120], P('dp', 'group', 'tensor'), may hold values from -6 to 6
- prefix_keys: bfloat16 [2, 1024, 1024], P('dp', 'group', 'tensor'), may hold values from -12 to 12
- prefix_values: bfloat16 [2, 1024, 1024], P('dp', 'group', 'tensor'), may hold values from -6 to 6
- advantages: float32 [2, 32], P('dp', 'group'), may hold values from -4 to 4
- lengths: int32 [2, 32], P('dp', 'group'), may hold values from 64 to 256, as said below
Outputs:
- grad_queries: bfloat16 [2, 32, 256, 5120], P('dp', 'group', None, 'tensor')
- grad_suffix_keys: bfloat16 [2, 32, 256, 1024], P('dp', 'group', None, 'tensor')
- grad_suffix_values: bfloat16 [2, 32, 256, 1024], P('dp', 'group', None, 'tensor')
- grad_prefix_keys: bfloat16 [2, 1024, 1024], P('dp', 'group', 'tensor')
- grad_prefix_values: bfloat16 [2, 1024, 1024], P('dp', 'group', 'tensor')
- grad_query_bias: float32 [5120], P('tensor')
- grad_kv_bias: float32 [2, 1024], P(None, 'tensor')
The draws below stay inside these ranges and needn't reach their ends.
Inputs may be any that keep to these rules, and one draw needn't show every extreme that they name: `lengths`: in every prompt some rollout has length 256.
All inputs are finite; a program needn't handle non-finite values.
Results may differ from the reference program's by a relative error of at most 0.02.
Values may be sent and summed in bfloat16 or wider, within the bound.
A program may use at most 64 MiB of HBM per device.

```python
import jax
import jax.numpy as jnp
from jax import lax

H = 40
KEY_VALUE_HEADS = 8
HEAD_SIZE = 128
RESP = 256
PROMPTS = 2
ROLLOUTS = 32
PREFIX = 1024


def draw_prefix_keys(key, part):
    key = jax.random.fold_in(key, 1)
    drawn = jnp.clip(jax.random.normal(key, (PROMPTS, PREFIX, KEY_VALUE_HEADS * HEAD_SIZE), jnp.float32), -6.0, 6.0)
    return drawn.astype(jnp.bfloat16)


def draw_queries(key, part):
    key = jax.random.fold_in(key, 2)
    drawn = jnp.clip(jax.random.normal(key, (PROMPTS, ROLLOUTS, RESP, H * HEAD_SIZE), jnp.float32), -6.0, 6.0)
    return drawn.astype(jnp.bfloat16)


def draw_lengths(key, part):
    key = jax.random.fold_in(key, 3)
    values = jax.random.randint(jax.random.fold_in(key, 1), (PROMPTS, ROLLOUTS), RESP // 4, RESP + 1)
    picks = jax.random.randint(jax.random.fold_in(key, 2), (PROMPTS,), 0, ROLLOUTS)
    rolls = jnp.arange(ROLLOUTS, dtype=jnp.int32)
    return jnp.where(rolls[None, :] == picks[:, None], RESP, values).astype(jnp.int32)


def shard_levels(key, extent, cuts, least, largest):
    loudness = 1.0
    for position, shards_of in cuts:
        draws = jax.random.uniform(jax.random.fold_in(jax.random.fold_in(key, 6), position), (shards_of,), jnp.float32, least / len(cuts), largest / len(cuts))
        loudness = loudness * jnp.repeat(jnp.exp(draws), extent[position] // shards_of).reshape((-1,) + (1,) * (len(extent) - 1 - position))
    return loudness


def gaussian(own_key, dims, scale, limit, cuts=(), held_as=jnp.bfloat16):
    factor_of = shard_levels(own_key, dims, cuts, -0.22, 0.18) if cuts else 1.0
    entries = jax.random.normal(own_key, dims, jnp.float32) * scale * factor_of
    return jnp.minimum(jnp.maximum(entries, -limit), limit).astype(held_as)


def setup_inputs(seed: int = 0) -> dict:
    splits = jax.random.split(jax.random.key(seed), 9)
    return {
        "queries": draw_queries(jax.random.fold_in(splits[8], 71), 0),
        "suffix_keys": gaussian(splits[1], (PROMPTS, ROLLOUTS, RESP, KEY_VALUE_HEADS * HEAD_SIZE), 1.0, 6.0, ((0, 2), (1, 32), (2, 4))),
        "suffix_values": gaussian(splits[2], (PROMPTS, ROLLOUTS, RESP, KEY_VALUE_HEADS * HEAD_SIZE), 1.0, 6.0, ((0, 2), (1, 32), (2, 4))),
        "d_out": gaussian(splits[3], (PROMPTS, ROLLOUTS, RESP, H * HEAD_SIZE), 1.0, 6.0, ((0, 2), (1, 32), (2, 4))),
        "prefix_keys": draw_prefix_keys(jax.random.fold_in(splits[8], 71), 0),
        "prefix_values": gaussian(splits[5], (PROMPTS, PREFIX, KEY_VALUE_HEADS * HEAD_SIZE), 1.0, 6.0, ((0, 2), (1, 32), (2, 4))),
        "advantages": gaussian(splits[6], (PROMPTS, ROLLOUTS), 1.0, 4.0, ((0, 2), (1, 32)), jnp.float32),
        "lengths": draw_lengths(jax.random.fold_in(splits[8], 71), 0),
    }


def rollout_pieces(query_matrix, suffix_key_block, suffix_value_block, output_gradient, rollout_advantage, suffix_length, prefix_key_block, prefix_value_block):
    ratio = H // KEY_VALUE_HEADS
    scale = HEAD_SIZE ** -0.5
    q5 = query_matrix.astype(jnp.float32).reshape(RESP, KEY_VALUE_HEADS, ratio, HEAD_SIZE)
    key_matrix = jnp.concatenate([prefix_key_block, suffix_key_block], axis=0).astype(jnp.float32).reshape(-1, KEY_VALUE_HEADS, HEAD_SIZE)
    value_matrix = jnp.concatenate([prefix_value_block, suffix_value_block], axis=0).astype(jnp.float32).reshape(-1, KEY_VALUE_HEADS, HEAD_SIZE)
    positions = jnp.arange(RESP, dtype=jnp.int32)
    valid = (positions < suffix_length).astype(jnp.float32)
    factor = (rollout_advantage / suffix_length.astype(jnp.float32)) * valid
    cot = (output_gradient.astype(jnp.float32) * factor[:, None]).astype(jnp.bfloat16)
    cot5 = cot.astype(jnp.float32).reshape(RESP, KEY_VALUE_HEADS, ratio, HEAD_SIZE)
    key_pos = jnp.arange(PREFIX + RESP, dtype=jnp.int32)
    offset = key_pos - PREFIX
    seen = (key_pos[None, :] < PREFIX) | ((offset[None, :] <= positions[:, None]) & (offset[None, :] < suffix_length))
    scores = jnp.einsum('tkgd,skd->kgts', q5, key_matrix) * scale
    scores = jnp.where(seen[None, None], scores, -jnp.inf)
    top = jnp.max(scores, axis=-1, keepdims=True)
    expd = jnp.exp(scores - top)
    probs = expd / jnp.sum(expd, axis=-1, keepdims=True)
    dprobs = jnp.einsum('tkgd,skd->kgts', cot5, value_matrix)
    delta = jnp.sum(probs * dprobs, axis=-1, keepdims=True)
    probs_b = lax.optimization_barrier(probs.astype(jnp.bfloat16)).astype(jnp.float32)
    dscores = lax.optimization_barrier((probs * (dprobs - delta)).astype(jnp.bfloat16)).astype(jnp.float32)
    query_gradient = scale * jnp.einsum('kgts,skd->tkgd', dscores, key_matrix)
    key_gradient = scale * jnp.einsum('kgts,tkgd->skd', dscores, q5)
    value_gradient = jnp.einsum('kgts,tkgd->skd', probs_b, cot5)
    return query_gradient, key_gradient, value_gradient


def reference(queries, suffix_keys, suffix_values, d_out, prefix_keys, prefix_values, advantages, lengths):
    cols = KEY_VALUE_HEADS * HEAD_SIZE
    grad_q_list = []
    grad_sk_list = []
    grad_sv_list = []
    grad_pk_list = []
    grad_pv_list = []
    qbias = jnp.zeros((H * HEAD_SIZE,), jnp.float32)
    kbias = jnp.zeros((cols,), jnp.float32)
    vbias = jnp.zeros((cols,), jnp.float32)
    for prompt in range(PROMPTS):
        prefix_key_block = prefix_keys[prompt]
        prefix_value_block = prefix_values[prompt]

        def step(carry, rollout_item):
            dk_pre, dv_pre, qb, kb, vb = carry
            query_matrix, suffix_key_block, suffix_value_block, output_gradient, rollout_advantage, suffix_length = rollout_item
            query_gradient, key_gradient, value_gradient = rollout_pieces(query_matrix, suffix_key_block, suffix_value_block, output_gradient, rollout_advantage, suffix_length, prefix_key_block, prefix_value_block)
            dk_pre = dk_pre + key_gradient[:PREFIX].reshape(PREFIX, cols)
            dv_pre = dv_pre + value_gradient[:PREFIX].reshape(PREFIX, cols)
            qb = qb + jnp.sum(query_gradient, axis=0).reshape(-1)
            kb = kb + jnp.sum(key_gradient[PREFIX:], axis=0).reshape(-1)
            vb = vb + jnp.sum(value_gradient[PREFIX:], axis=0).reshape(-1)
            outs = (query_gradient.reshape(RESP, H * HEAD_SIZE).astype(jnp.bfloat16),
                    key_gradient[PREFIX:].reshape(RESP, cols).astype(jnp.bfloat16),
                    value_gradient[PREFIX:].reshape(RESP, cols).astype(jnp.bfloat16))
            return (dk_pre, dv_pre, qb, kb, vb), outs

        init = (jnp.zeros((PREFIX, cols), jnp.float32), jnp.zeros((PREFIX, cols), jnp.float32),
                qbias, kbias, vbias)
        items = (queries[prompt], suffix_keys[prompt], suffix_values[prompt], d_out[prompt],
                 advantages[prompt], lengths[prompt])
        carry, outs = lax.scan(step, init, items)
        dk_pre, dv_pre, qbias, kbias, vbias = carry
        grad_q_list.append(outs[0])
        grad_sk_list.append(outs[1])
        grad_sv_list.append(outs[2])
        grad_pk_list.append(dk_pre.astype(jnp.bfloat16))
        grad_pv_list.append(dv_pre.astype(jnp.bfloat16))
    return (jnp.stack(grad_q_list), jnp.stack(grad_sk_list), jnp.stack(grad_sv_list),
            jnp.stack(grad_pk_list), jnp.stack(grad_pv_list), qbias, jnp.stack([kbias, vbias]))
```

```python
import math

import jax
import jax.numpy as jnp
from jax import lax
from jax.experimental import pallas as pl
from jax.experimental.pallas import tpu as pltpu
from jax.sharding import PartitionSpec as P

H = 40
KEY_VALUE_HEADS = 8
D = 128
RATIO = H // KEY_VALUE_HEADS
NX = 4
NY = 4
NZ = 4
KV = KEY_VALUE_HEADS // NX
TOK = 64
RESP = NX * TOK
QC = RATIO * D
PRE = 1024
KEYS = PRE + RESP
PIECE = PRE // (2 * NY * NZ)
YROWS = NZ * PIECE
HALF = NY * YROWS
QT = RATIO * RESP
SCALE = D ** -0.5
C2 = SCALE * math.log2(math.e)
MESH = pl.DeviceIdType.MESH
F32 = jnp.float32
BF16 = jnp.bfloat16


def nt(a, b):
    return lax.dot_general(a, b, (((1,), (1,)), ((), ())), preferred_element_type=F32)


def nn(a, b):
    return lax.dot_general(a, b, (((1,), (0,)), ((), ())), preferred_element_type=F32)


def fold(a, op):
    return op(a.reshape(a.shape[0] // 8, 8, a.shape[1]), axis=0)


def kernel(
    q_in, ks_in, vs_in, do_in, pk_in, pv_in, adv_ref, len_ref,
    dq_out, dks_out, dvs_out, dpk_out, dpv_out, qb_out, kvb_out,
    q_all, do_all, k_all, v_all, k_t, q_st, c_st, s_buf, dp_buf, p_all, ds_all,
    dq_v, dks_v, dvs_v, rs_snd, rs_sib, rs_own, rs_ysnd, rs_y, rs_zsum, rs_zsnd, rs_z, dpk_v, dpv_v,
    b_own, b_sib, b_y, b_z, qb_v, kvb_v,
    xs, xr, xl, gzs, gzr, gzl, gys, gyr, gss, gsr,
    r0s, r0r, r1s, r1r, r2s, r2r, bs0, br0, bs1, br1, bs2, br2, osem,
):
    g = lax.axis_index("group")
    x = lax.axis_index("tensor")
    dp = lax.axis_index("dp")
    core = lax.rem(g, 2)
    zh = lax.rem(g // 2, NZ)
    y = g // (2 * NZ)
    sib = {"group": g + 1 - 2 * core}

    def xdev(d):
        return {"tensor": lax.rem(x + d, NX)}

    def ydev(d):
        return {"group": lax.rem(y + d, NY) * (2 * NZ) + zh * 2 + core}

    def zdev(d):
        return {"group": y * (2 * NZ) + lax.rem(zh + d, NZ) * 2 + core}

    zpos = zh * 2 + dp

    def zzdev(d):
        p = lax.rem(zpos + d, 2 * NZ)
        return {"group": y * (2 * NZ) + (p // 2) * 2 + core, "dp": lax.rem(p, 2)}

    def remote(src, dst, ss, rs, dev):
        return pltpu.make_async_remote_copy(
            src_ref=src, dst_ref=dst, send_sem=ss, recv_sem=rs, device_id=dev, device_id_type=MESH
        )

    barrier = pltpu.get_barrier_semaphore()
    peers = [sib] + [xdev(d) for d in range(1, NX)] + [ydev(d) for d in range(1, NY)]
    peers += [zzdev(d) for d in range(1, 2 * NZ)]
    for dev in peers:
        pl.semaphore_signal(barrier, inc=1, device_id=dev, device_id_type=MESH)

    def cols(owner, kv):
        return pl.ds(pl.multiple_of(owner * (KV * QC) + kv * QC, D), QC)

    def kcols(owner):
        return pl.ds(pl.multiple_of(owner * (KV * D), D), KV * D)

    def trow(owner, base=0):
        return pl.ds(pl.multiple_of(base + owner * TOK, TOK), TOK)

    def xsrc(kind, owner):
        if kind in (0, 4):
            return q_in.at[:, cols(owner, kind // 4)]
        if kind in (1, 5):
            return do_in.at[:, cols(owner, kind // 4)]
        return (ks_in if kind == 2 else vs_in).at[:, kcols(owner)]

    def xdst(kind, source):
        if kind in (0, 4):
            return q_all.at[kind // 4, trow(source)]
        if kind in (1, 5):
            return do_all.at[kind // 4, trow(source)]
        return (k_all if kind == 2 else v_all).at[trow(source, PRE)]

    def xsend(kind, d):
        return remote(
            xsrc(kind, lax.rem(x + d, NX)), xdst(kind, x), xs.at[kind, d - 1], xr.at[kind, d - 1], xdev(d)
        )

    def xrecv(kind, d):
        dst = xdst(kind, lax.rem(x + NX - d, NX))
        return remote(dst, dst, xs.at[kind, d - 1], xr.at[kind, d - 1], xdev(d))

    def xlocal(kind):
        return pltpu.make_async_copy(xsrc(kind, x), xdst(kind, x), xl.at[kind])

    def prow(c, yy, zz, n=PIECE):
        return pl.ds(pl.multiple_of(c * HALF + yy * YROWS + zz * PIECE, PIECE), n)

    full = (k_all, v_all)
    piece = (pk_in, pv_in)

    def gz(kind, d):
        return remote(piece[kind], full[kind].at[prow(core, y, zh)], gzs.at[kind, d - 1], gzr.at[kind, d - 1], zdev(d))

    def gz_recv(kind, d):
        dst = full[kind].at[prow(core, y, lax.rem(zh + NZ - d, NZ))]
        return remote(dst, dst, gzs.at[kind, d - 1], gzr.at[kind, d - 1], zdev(d))

    def gz_local(kind):
        return pltpu.make_async_copy(piece[kind], full[kind].at[prow(core, y, zh)], gzl.at[kind])

    def gy(kind, d):
        blk = full[kind].at[prow(core, y, 0, YROWS)]
        return remote(blk, blk, gys.at[kind, d - 1], gyr.at[kind, d - 1], ydev(d))

    def gy_recv(kind, d):
        dst = full[kind].at[prow(core, lax.rem(y + NY - d, NY), 0, YROWS)]
        return remote(dst, dst, gys.at[kind, d - 1], gyr.at[kind, d - 1], ydev(d))

    def gs(kind, d):
        blk = full[kind].at[prow(core, lax.rem(y + NY - d, NY), 0, YROWS)]
        return remote(blk, blk, gss.at[kind, d], gsr.at[kind, d], sib)

    def gs_recv(kind, d):
        dst = full[kind].at[prow(1 - core, lax.rem(y + NY - d, NY), 0, YROWS)]
        return remote(dst, dst, gss.at[kind, d], gsr.at[kind, d], sib)

    for kind in (0, 1):
        gz_local(kind).start()
    for kind in range(6):
        xlocal(kind).start()

    pl.semaphore_wait(barrier, len(peers))

    for kind in (0, 1):
        for d in range(1, NZ):
            gz(kind, d).start()
    for kind in (0, 2, 1, 3, 4, 5):
        for d in range(1, NX):
            xsend(kind, d).start()

    for kind in (0, 1):
        gz_local(kind).wait()
        for d in range(1, NZ):
            gz_recv(kind, d).wait_recv()
        for d in range(1, NY):
            gy(kind, d).start()
        gs(kind, 0).start()
    for kind in (0, 1):
        for d in range(1, NY):
            gy_recv(kind, d).wait_recv()
            gs(kind, d).start()
    for kind in (0, 1):
        for d in range(NY):
            gs_recv(kind, d).wait_recv()

    def arrive(kinds):
        for kind in kinds:
            xlocal(kind).wait()
            for d in range(1, NX):
                xrecv(kind, d).wait_recv()

    length = len_ref[0, 0]
    tok = lax.broadcasted_iota(jnp.int32, (RESP, 1), 0)
    weight = jnp.full((RESP, 1), adv_ref[0, 0], F32) / jnp.full((RESP, 1), length.astype(F32), F32)
    factor = jnp.where(tok < length, weight, 0.0)

    def seen():
        s = lax.broadcasted_iota(jnp.int32, (RESP, RESP), 0)
        t = lax.broadcasted_iota(jnp.int32, (RESP, RESP), 1)
        return (s <= t) & (s < length)

    nblk = KEYS // RESP

    def head(kv, h):
        lanes = slice(kv * D, (kv + 1) * D)
        rows = pl.ds(pl.multiple_of(h * RESP, RESP), RESP)
        qh = q_st[kv, rows]
        ch = c_st[kv, rows]
        top = None
        for b in range(nblk):
            kr = slice(b * RESP, (b + 1) * RESP)
            s = nt(k_all[kr, lanes], qh)
            if b == nblk - 1:
                s = jnp.where(seen(), s, -1e30)
            s_buf[kr] = s
            m = fold(s, jnp.max)
            top = m if top is None else jnp.maximum(top, m)
        top = jnp.max(top, axis=0, keepdims=True) * C2
        total = accum = None
        for b in range(nblk):
            kr = slice(b * RESP, (b + 1) * RESP)
            dpr = nt(v_all[kr, lanes], ch)
            e = jnp.exp2(s_buf[kr] * C2 - top)
            s_buf[kr] = e
            dp_buf[kr] = dpr
            t1 = fold(e, jnp.sum)
            t2 = fold(e * dpr, jnp.sum)
            total = t1 if total is None else total + t1
            accum = t2 if accum is None else accum + t2
        total = jnp.sum(total, axis=0, keepdims=True)
        accum = jnp.sum(accum, axis=0, keepdims=True)
        inv = 1.0 / total
        delta = accum * inv
        for b in range(nblk):
            kr = slice(b * RESP, (b + 1) * RESP)
            p = s_buf[kr] * inv
            p_all[kr, rows] = p.astype(BF16)
            ds_all[kr, rows] = (p * (dp_buf[kr] - delta)).astype(BF16)

    def rsib(kv):
        return remote(rs_snd.at[kv], rs_sib.at[kv], r0s.at[kv], r0r.at[kv], sib)

    def ry(kv, d):
        src = rs_ysnd.at[kv, pl.ds(pl.multiple_of(lax.rem(y + d, NY) * YROWS, YROWS), YROWS)]
        return remote(src, rs_y.at[kv, d - 1], r1s.at[kv, d - 1], r1r.at[kv, d - 1], ydev(d))

    def rz(kv, d):
        src = rs_zsnd.at[kv, pl.ds(pl.multiple_of(lax.rem(zh + d, NZ) * PIECE, PIECE), PIECE)]
        return remote(src, rs_z.at[kv, d - 1], r2s.at[kv, d - 1], r2r.at[kv, d - 1], zdev(d))

    def reduce_sib(kv):
        rsib(kv).wait_recv()
        own = rs_own[...] + rs_sib[kv].astype(F32)
        rs_own[...] = own
        rs_ysnd[kv] = own.astype(BF16)
        for d in range(1, NY):
            ry(kv, d).start()

    def reduce_y(kv):
        acc = rs_own[pl.ds(pl.multiple_of(y * YROWS, YROWS), YROWS)]
        for d in range(1, NY):
            ry(kv, d).wait_recv()
            acc = acc + rs_y[kv, d - 1].astype(F32)
        rs_zsum[...] = acc
        rs_zsnd[kv] = acc.astype(BF16)
        for d in range(1, NZ):
            rz(kv, d).start()

    def reduce_z(kv):
        acc = rs_zsum[pl.ds(pl.multiple_of(zh * PIECE, PIECE), PIECE)]
        for d in range(1, NZ):
            rz(kv, d).wait_recv()
            acc = acc + rs_z[kv, d - 1].astype(F32)
        dpk_v[:, kv * D : (kv + 1) * D] = acc[:, :D].astype(BF16)
        dpv_v[:, kv * D : (kv + 1) * D] = acc[:, D:].astype(BF16)

    def span(kv, lo, hi):
        def step(h, carry):
            head(kv, h)
            return carry

        lax.fori_loop(lo, hi, step, 0)

    b_own[...] = jnp.zeros_like(b_own)

    for kv in range(KV):
        lanes = slice(kv * D, (kv + 1) * D)
        arrive((0, 1, 2, 3) if kv == 0 else (4, 5))
        for h in range(RATIO):
            rows = slice(h * RESP, (h + 1) * RESP)
            q_st[kv, rows] = q_all[kv, :, h * D : (h + 1) * D]
            c_st[kv, rows] = (do_all[kv, :, h * D : (h + 1) * D].astype(F32) * factor).astype(BF16)
        k_t[...] = k_all[:, lanes].T
        if kv == 0:
            span(kv, 0, RATIO)
        else:
            span(kv, 0, 1)
            reduce_sib(kv - 1)
            span(kv, 1, 3)
            reduce_y(kv - 1)
            span(kv, 3, RATIO)
            reduce_z(kv - 1)
        other = pl.ds(pl.multiple_of((1 - core) * HALF, HALF), HALF)
        mine = pl.ds(pl.multiple_of(core * HALF, HALF), HALF)
        rs_snd[kv, :, :D] = (nn(ds_all[other], q_st[kv]) * SCALE).astype(BF16)
        rs_snd[kv, :, D:] = nn(p_all[other], c_st[kv]).astype(BF16)
        rsib(kv).start()
        rs_own[:, :D] = nn(ds_all[mine], q_st[kv]) * SCALE
        rs_own[:, D:] = nn(p_all[mine], c_st[kv])
        if kv == KV - 1:
            reduce_sib(kv)
        dks = nn(ds_all[PRE:], q_st[kv]) * SCALE
        dvs = nn(p_all[PRE:], c_st[kv])
        dks_v[:, lanes] = dks.astype(BF16)
        dvs_v[:, lanes] = dvs.astype(BF16)
        b_own[KV * RATIO + kv : KV * RATIO + kv + 1] = jnp.sum(dks, axis=0, keepdims=True)
        b_own[KV * RATIO + KV + kv : KV * RATIO + KV + kv + 1] = jnp.sum(dvs, axis=0, keepdims=True)
        for h in range(RATIO):
            dqh = (nn(k_t[...], ds_all[:, h * RESP : (h + 1) * RESP]) * SCALE).T
            r = kv * RATIO + h
            dq_v[:, r * D : (r + 1) * D] = dqh.astype(BF16)
            b_own[r : r + 1] = jnp.sum(dqh, axis=0, keepdims=True)

    outs = [
        pltpu.make_async_copy(dq_v, dq_out, osem.at[0]),
        pltpu.make_async_copy(dks_v, dks_out, osem.at[1]),
        pltpu.make_async_copy(dvs_v, dvs_out, osem.at[2]),
    ]
    for copy in outs:
        copy.start()

    bsib = remote(b_own, b_sib, bs0, br0, sib)
    bsib.start()
    reduce_y(KV - 1)
    bsib.wait_recv()
    b_y[pl.ds(y, 1)] = (b_own[...] + b_sib[...])[None]

    def by(d):
        return remote(b_y.at[y], b_y.at[y], bs1.at[d - 1], br1.at[d - 1], ydev(d))

    def by_recv(d):
        dst = b_y.at[lax.rem(y + NY - d, NY)]
        return remote(dst, dst, bs1.at[d - 1], br1.at[d - 1], ydev(d))

    for d in range(1, NY):
        by(d).start()
    reduce_z(KV - 1)
    for d in range(1, NY):
        by_recv(d).wait_recv()
    acc = b_y[0]
    for i in range(1, NY):
        acc = acc + b_y[i]
    b_z[pl.ds(zpos, 1)] = acc[None]

    def bz(d):
        return remote(b_z.at[zpos], b_z.at[zpos], bs2.at[d - 1], br2.at[d - 1], zzdev(d))

    def bz_recv(d):
        dst = b_z.at[lax.rem(zpos + 2 * NZ - d, 2 * NZ)]
        return remote(dst, dst, bs2.at[d - 1], br2.at[d - 1], zzdev(d))

    for d in range(1, 2 * NZ):
        bz(d).start()
    tail = [
        pltpu.make_async_copy(dpk_v, dpk_out, osem.at[3]),
        pltpu.make_async_copy(dpv_v, dpv_out, osem.at[4]),
    ]
    for copy in tail:
        copy.start()
    for d in range(1, 2 * NZ):
        bz_recv(d).wait_recv()
    acc = b_z[0]
    for i in range(1, 2 * NZ):
        acc = acc + b_z[i]
    nq = KV * RATIO
    qb_v[...] = acc[:nq]
    for kv in range(KV):
        kvb_v[0:1, kv * D : (kv + 1) * D] = acc[nq + kv : nq + kv + 1]
        kvb_v[1:2, kv * D : (kv + 1) * D] = acc[nq + KV + kv : nq + KV + kv + 1]
    tail2 = [
        pltpu.make_async_copy(qb_v, qb_out, osem.at[5]),
        pltpu.make_async_copy(kvb_v, kvb_out, osem.at[6]),
    ]
    for copy in tail2:
        copy.start()

    for kind in range(6):
        for d in range(1, NX):
            xsend(kind, d).wait_send()
    for kind in (0, 1):
        for d in range(1, NZ):
            gz(kind, d).wait_send()
        for d in range(1, NY):
            gy(kind, d).wait_send()
        for d in range(NY):
            gs(kind, d).wait_send()
    for kv in range(KV):
        rsib(kv).wait_send()
        for d in range(1, NY):
            ry(kv, d).wait_send()
        for d in range(1, NZ):
            rz(kv, d).wait_send()
    bsib.wait_send()
    for d in range(1, NY):
        by(d).wait_send()
    for d in range(1, 2 * NZ):
        bz(d).wait_send()
    for copy in outs + tail + tail2:
        copy.wait()


def local(queries, suffix_keys, suffix_values, d_out, prefix_keys, prefix_values, advantages, lengths):
    sds = jax.ShapeDtypeStruct
    dma = pltpu.SemaphoreType.DMA
    hbm = pl.BlockSpec(memory_space=pl.ANY)
    smem = pl.BlockSpec(memory_space=pltpu.SMEM)
    nb = KV * RATIO
    vm = pltpu.VMEM
    out = pl.pallas_call(
        kernel,
        out_shape=(
            sds((RESP, KV * QC), BF16),
            sds((RESP, KV * D), BF16),
            sds((RESP, KV * D), BF16),
            sds((PIECE, KV * D), BF16),
            sds((PIECE, KV * D), BF16),
            sds((nb, D), F32),
            sds((2, KV * D), F32),
        ),
        in_specs=[hbm] * 6 + [smem] * 2,
        out_specs=(hbm,) * 7,
        scratch_shapes=[
            vm((KV, RESP, QC), BF16), vm((KV, RESP, QC), BF16),
            vm((KEYS, KV * D), BF16), vm((KEYS, KV * D), BF16),
            vm((D, KEYS), BF16),
            vm((KV, QT, D), BF16), vm((KV, QT, D), BF16),
            vm((KEYS, RESP), F32), vm((KEYS, RESP), F32),
            vm((KEYS, QT), BF16), vm((KEYS, QT), BF16),
            vm((RESP, KV * QC), BF16), vm((RESP, KV * D), BF16), vm((RESP, KV * D), BF16),
            vm((KV, HALF, 2 * D), BF16), vm((KV, HALF, 2 * D), BF16), vm((HALF, 2 * D), F32),
            vm((KV, HALF, 2 * D), BF16), vm((KV, NY - 1, YROWS, 2 * D), BF16),
            vm((YROWS, 2 * D), F32), vm((KV, YROWS, 2 * D), BF16),
            vm((KV, NZ - 1, PIECE, 2 * D), BF16), vm((PIECE, KV * D), BF16), vm((PIECE, KV * D), BF16),
            vm((16, D), F32), vm((16, D), F32), vm((NY, 16, D), F32), vm((2 * NZ, 16, D), F32),
            vm((nb, D), F32), vm((2, KV * D), F32),
            dma((6, NX - 1)), dma((6, NX - 1)), dma((6,)),
            dma((2, NZ - 1)), dma((2, NZ - 1)), dma((2,)),
            dma((2, NY - 1)), dma((2, NY - 1)), dma((2, NY)), dma((2, NY)),
            dma((KV,)), dma((KV,)), dma((KV, NY - 1)), dma((KV, NY - 1)), dma((KV, NZ - 1)), dma((KV, NZ - 1)),
            dma, dma, dma((NY - 1,)), dma((NY - 1,)), dma((2 * NZ - 1,)), dma((2 * NZ - 1,)),
            dma((7,)),
        ],
        compiler_params=pltpu.CompilerParams(
            collective_id=0, has_side_effects=True, vmem_limit_bytes=48 * 1024 * 1024
        ),
        name="grouped_attention_backward",
    )(
        queries[0, 0], suffix_keys[0, 0], suffix_values[0, 0], d_out[0, 0],
        prefix_keys[0], prefix_values[0], advantages, lengths,
    )
    dq, dks, dvs, dpk, dpv, qb, kvb = out
    return (dq[None, None], dks[None, None], dvs[None, None], dpk[None], dpv[None], qb.reshape(-1), kvb)


def solution(mesh):
    in_specs = (
        P("dp", "group", "tensor", None),
        P("dp", "group", "tensor", None),
        P("dp", "group", "tensor", None),
        P("dp", "group", "tensor", None),
        P("dp", "group", "tensor"),
        P("dp", "group", "tensor"),
        P("dp", "group"),
        P("dp", "group"),
    )
    out_specs = (
        P("dp", "group", None, "tensor"),
        P("dp", "group", None, "tensor"),
        P("dp", "group", None, "tensor"),
        P("dp", "group", "tensor"),
        P("dp", "group", "tensor"),
        P("tensor"),
        P(None, "tensor"),
    )
    return jax.shard_map(local, mesh=mesh, in_specs=in_specs, out_specs=out_specs, check_vma=False)
```

```python
import math

import jax
import jax.numpy as jnp
from jax import lax
from jax.experimental import pallas as pl
from jax.experimental.pallas import tpu as pltpu
from jax.sharding import PartitionSpec as P

H = 40
KEY_VALUE_HEADS = 8
D = 128
RATIO = H // KEY_VALUE_HEADS
NX = 4
NY = 4
NZ = 4
KV = KEY_VALUE_HEADS // NX
TOK = 64
RESP = NX * TOK
QC = RATIO * D
PRE = 1024
KEYS = PRE + RESP
PIECE = PRE // (2 * NY * NZ)
YROWS = NZ * PIECE
HALF = NY * YROWS
QT = RATIO * RESP
SCALE = D ** -0.5
C2 = SCALE * math.log2(math.e)
MESH = pl.DeviceIdType.MESH
F32 = jnp.float32
BF16 = jnp.bfloat16


def nt(a, b):
    return lax.dot_general(a, b, (((1,), (1,)), ((), ())), preferred_element_type=F32)


def nn(a, b):
    return lax.dot_general(a, b, (((1,), (0,)), ((), ())), preferred_element_type=F32)


def fold(a, op):
    return op(a.reshape(a.shape[0] // 8, 8, a.shape[1]), axis=0)


def kernel(
    q_in, ks_in, vs_in, do_in, pk_in, pv_in, adv_ref, len_ref,
    dq_out, dks_out, dvs_out, dpk_out, dpv_out, qb_out, kvb_out,
    q_st, do_st, c_st, kv_all, k_t, s_buf, dp_buf, p_all, ds_all,
    dq_v, dks_v, dvs_v, rs_snd, rs_sib, rs_own, rs_ysnd, rs_y, rs_zsum, rs_zsnd, rs_z, dpk_v, dpv_v,
    b_y, b_z, qb_v, kvb_v,
    xs, xr, kvs, kvr, gl, gzs, gzr, gys, gyr, gss, gsr,
    r0s, r0r, r1s, r1r, r2s, r2r, bs1, br1, bs2, br2, osem,
):
    g = lax.axis_index("group")
    x = lax.axis_index("tensor")
    dp = lax.axis_index("dp")
    core = lax.rem(g, 2)
    zh = lax.rem(g // 2, NZ)
    y = g // (2 * NZ)
    sib = {"group": g + 1 - 2 * core}

    def xdev(d):
        return {"tensor": lax.rem(x + d, NX)}

    def ydev(d):
        return {"group": lax.rem(y + d, NY) * (2 * NZ) + zh * 2 + core}

    def zdev(d):
        return {"group": y * (2 * NZ) + lax.rem(zh + d, NZ) * 2 + core}

    ypos = y * 2 + core
    zpos = zh * 2 + dp

    def yydev(d):
        p = lax.rem(ypos + d, 2 * NY)
        return {"group": (p // 2) * (2 * NZ) + zh * 2 + lax.rem(p, 2)}

    def zzdev(d):
        p = lax.rem(zpos + d, 2 * NZ)
        return {"group": y * (2 * NZ) + (p // 2) * 2 + core, "dp": lax.rem(p, 2)}

    def remote(src, dst, ss, rs, dev):
        return pltpu.make_async_remote_copy(
            src_ref=src, dst_ref=dst, send_sem=ss, recv_sem=rs, device_id=dev, device_id_type=MESH
        )

    def await_recv(ref, sem):
        remote(ref, ref, osem.at[0], sem, sib).wait_recv()

    def await_send(ref, sem):
        remote(ref, ref, sem, osem.at[0], sib).wait_send()

    barrier = pltpu.get_barrier_semaphore()
    peers = [xdev(d) for d in range(1, NX)] + [yydev(d) for d in range(1, 2 * NY)]
    peers += [zzdev(d) for d in range(1, 2 * NZ)]
    for dev in peers:
        pl.semaphore_signal(barrier, inc=1, device_id=dev, device_id_type=MESH)

    def xsrc(kind, owner, r):
        return (q_in, do_in)[kind].at[:, pl.ds(pl.multiple_of((owner * KV * RATIO + r) * D, D), D)]

    def xdst(kind, source, r):
        return (q_st, do_st)[kind].at[pl.ds(pl.multiple_of(r * RESP + source * TOK, TOK), TOK)]

    def ksrc(kind, owner, kv):
        return (ks_in, vs_in)[kind].at[:, pl.ds(pl.multiple_of((owner * KV + kv) * D, D), D)]

    def kdst(kind, source, kv):
        return kv_all.at[kv, pl.ds(pl.multiple_of(PRE + source * TOK, TOK), TOK), kind * D : (kind + 1) * D]

    def start_head(r):
        for kind in (0, 1):
            for d in (2, 1, 3):
                src = xsrc(kind, lax.rem(x + d, NX), r)
                remote(src, xdst(kind, x, r), xs.at[kind], xr.at[kind, r], xdev(d)).start()

    def start_keys(kv):
        for kind in (0, 1):
            for d in (2, 1, 3):
                src = ksrc(kind, lax.rem(x + d, NX), kv)
                remote(src, kdst(kind, x, kv), kvs, kvr.at[kv], xdev(d)).start()

    def prow(c, zz, yy, n=PIECE):
        return pl.ds(pl.multiple_of(c * HALF + zz * YROWS + yy * PIECE, PIECE), n)

    def from_z(e):
        return lax.rem(zh + NZ - e, NZ)

    def gather_z(kv):
        own = kv_all.at[kv, prow(core, zh, y)]
        for d in (2, 1, 3):
            remote(own, own, gzs.at[kv], gzr.at[kv, d - 1], zdev(d)).start()

    def gather_y(kv, e):
        blk = kv_all.at[kv, prow(core, from_z(e), y)]
        if e > 0:
            await_recv(blk, gzr.at[kv, e - 1])
        for d in (2, 1, 3):
            remote(blk, blk, gys.at[kv], gyr.at[kv, e], ydev(d)).start()

    def gather_sib(kv, e):
        await_recv(kv_all.at[kv, 0 : (NY - 1) * PIECE], gyr.at[kv, e])
        blk = kv_all.at[kv, prow(core, from_z(e), 0, YROWS)]
        remote(blk, blk, gss.at[kv], gsr.at[kv], sib).start()

    def gather_done(kv):
        await_recv(kv_all.at[kv, 0:HALF], gsr.at[kv])

    for kv in range(KV):
        for kind in (0, 1):
            dst = kv_all.at[kv, prow(core, zh, y), kind * D : (kind + 1) * D]
            pltpu.make_async_copy((pk_in, pv_in)[kind].at[:, kv * D : (kv + 1) * D], dst, gl.at[kv]).start()
    for kv in range(KV):
        await_recv(kv_all.at[kv, 0:PIECE], gl.at[kv])

    pl.semaphore_wait(barrier, len(peers))

    gather_z(0)
    gather_y(0, 0)
    start_head(0)
    start_keys(0)
    gather_z(1)
    gather_y(1, 0)
    for h in range(1, RATIO):
        start_head(h)
    for r in range(KV * RATIO):
        for kind in (0, 1):
            pltpu.make_async_copy(xsrc(kind, x, r), xdst(kind, x, r), xr.at[kind, r]).start()
    for kv in range(KV):
        for kind in (0, 1):
            pltpu.make_async_copy(ksrc(kind, x, kv), kdst(kind, x, kv), kvr.at[kv]).start()
    order = (1, 3, 2)
    for e in order:
        gather_y(0, e)
    start_keys(1)
    start_head(RATIO)
    for e in order:
        gather_y(1, e)
    start_head(RATIO + 1)
    for e in (0,) + order:
        gather_sib(0, e)
    for h in range(2, RATIO):
        start_head(RATIO + h)
    gather_done(0)

    length = len_ref[0, 0]
    tok = lax.broadcasted_iota(jnp.int32, (RESP, 1), 0)
    weight = jnp.full((RESP, 1), adv_ref[0, 0], F32) / jnp.full((RESP, 1), length.astype(F32), F32)
    factor = jnp.where(tok < length, weight, 0.0)

    def seen():
        s = lax.broadcasted_iota(jnp.int32, (RESP, RESP), 0)
        t = lax.broadcasted_iota(jnp.int32, (RESP, RESP), 1)
        return (s <= t) & (s < length)

    nblk = KEYS // RESP

    def head(kv, h):
        rows = pl.ds(pl.multiple_of(h * RESP, RESP), RESP)
        r = kv * RATIO + h
        all_rows = pl.ds(pl.multiple_of(r * RESP, RESP), RESP)
        for kind in (0, 1):
            await_recv((q_st, do_st)[kind].at[all_rows], xr.at[kind, r])
        qh = q_st[all_rows]
        ch = (do_st[all_rows].astype(F32) * factor).astype(BF16)
        c_st[all_rows] = ch
        top = None
        for b in range(nblk):
            kr = slice(b * RESP, (b + 1) * RESP)
            s = nt(kv_all[kv, kr, :D], qh)
            if b == nblk - 1:
                s = jnp.where(seen(), s, -1e30)
            s_buf[kr] = s
            m = fold(s, jnp.max)
            top = m if top is None else jnp.maximum(top, m)
        top = jnp.max(top, axis=0, keepdims=True) * C2
        total = accum = None
        for b in range(nblk):
            kr = slice(b * RESP, (b + 1) * RESP)
            dpr = nt(kv_all[kv, kr, D:], ch)
            e = jnp.exp2(s_buf[kr] * C2 - top)
            s_buf[kr] = e
            dp_buf[kr] = dpr
            t1 = fold(e, jnp.sum)
            t2 = fold(e * dpr, jnp.sum)
            total = t1 if total is None else total + t1
            accum = t2 if accum is None else accum + t2
        total = jnp.sum(total, axis=0, keepdims=True)
        accum = jnp.sum(accum, axis=0, keepdims=True)
        inv = 1.0 / total
        delta = accum * inv
        for b in range(nblk):
            kr = slice(b * RESP, (b + 1) * RESP)
            p = s_buf[kr] * inv
            p_all[kr, rows] = p.astype(BF16)
            ds_all[kr, rows] = (p * (dp_buf[kr] - delta)).astype(BF16)

    def rsib(kv):
        return remote(rs_snd.at[kv], rs_sib.at[kv], r0s.at[kv], r0r.at[kv], sib)

    far = (2, 1, 3, 0)

    def to_z(e):
        return lax.rem(zh + e, NZ)

    def zrows(e):
        return pl.ds(pl.multiple_of(to_z(e) * YROWS, YROWS), YROWS)

    def zyrows(e, d):
        return pl.ds(pl.multiple_of(to_z(e) * YROWS + lax.rem(y + d, NY) * PIECE, PIECE), PIECE)

    def reduce_sib(kv):
        rsib(kv).wait_recv()
        for e in far:
            own = rs_own[zrows(e)] + rs_sib[kv, zrows(e)].astype(F32)
            rs_own[zrows(e)] = own
            rs_ysnd[kv, zrows(e)] = own.astype(BF16)
            for d in (2, 1, 3):
                src = rs_ysnd.at[kv, zyrows(e, d)]
                remote(src, rs_y.at[kv, e, d - 1], r1s.at[kv], r1r.at[kv, e], ydev(d)).start()

    def reduce_y(kv):
        for e in far:
            await_recv(rs_y.at[kv, e], r1r.at[kv, e])
            acc = rs_own[zyrows(e, 0)]
            for d in range(1, NY):
                acc = acc + rs_y[kv, e, d - 1].astype(F32)
            if e == 0:
                rs_zsum[...] = acc
            else:
                rs_zsnd[kv, e - 1] = acc.astype(BF16)
                remote(rs_zsnd.at[kv, e - 1], rs_z.at[kv, e - 1], r2s.at[kv], r2r.at[kv], zdev(e)).start()

    def reduce_z(kv):
        await_recv(rs_z.at[kv], r2r.at[kv])
        acc = rs_zsum[...]
        for d in range(1, NZ):
            acc = acc + rs_z[kv, d - 1].astype(F32)
        dpk_v[:, kv * D : (kv + 1) * D] = acc[:, :D].astype(BF16)
        dpv_v[:, kv * D : (kv + 1) * D] = acc[:, D:].astype(BF16)

    def span(kv, lo, hi):
        def step(h, carry):
            head(kv, h)
            return carry

        lax.fori_loop(lo, hi, step, 0)

    nb = KV * RATIO
    biases = [None] * 16
    outs = []
    for kv in range(KV):
        lanes = slice(kv * D, (kv + 1) * D)
        if kv > 0:
            gather_done(kv)
        await_recv(kv_all.at[kv, PRE:KEYS], kvr.at[kv])
        k_t[...] = kv_all[kv, :, :D].T
        if kv == 0:
            span(kv, 0, 1)
            for e in (0,) + order:
                gather_sib(1, e)
            span(kv, 1, RATIO)
        else:
            span(kv, 0, 1)
            reduce_sib(kv - 1)
            span(kv, 1, 3)
            reduce_y(kv - 1)
            span(kv, 3, RATIO)
            reduce_z(kv - 1)
        qs = slice(kv * QT, (kv + 1) * QT)
        other = pl.ds(pl.multiple_of((1 - core) * HALF, HALF), HALF)
        mine = pl.ds(pl.multiple_of(core * HALF, HALF), HALF)
        rs_snd[kv, :, :D] = (nn(ds_all[other], q_st[qs]) * SCALE).astype(BF16)
        rs_snd[kv, :, D:] = nn(p_all[other], c_st[qs]).astype(BF16)
        rsib(kv).start()
        rs_own[:, :D] = nn(ds_all[mine], q_st[qs]) * SCALE
        rs_own[:, D:] = nn(p_all[mine], c_st[qs])
        if kv == KV - 1:
            reduce_sib(kv)
        dks = nn(ds_all[PRE:], q_st[qs]) * SCALE
        dvs = nn(p_all[PRE:], c_st[qs])
        dks_v[:, lanes] = dks.astype(BF16)
        dvs_v[:, lanes] = dvs.astype(BF16)
        b_y[ypos, nb + kv : nb + kv + 1] = jnp.sum(dks, axis=0, keepdims=True)
        b_y[ypos, nb + KV + kv : nb + KV + kv + 1] = jnp.sum(dvs, axis=0, keepdims=True)
        for h in range(RATIO):
            dqh = (nn(k_t[...], ds_all[:, h * RESP : (h + 1) * RESP]) * SCALE).T
            r = kv * RATIO + h
            dq_v[:, r * D : (r + 1) * D] = dqh.astype(BF16)
            b_y[ypos, r : r + 1] = jnp.sum(dqh, axis=0, keepdims=True)
        copy = pltpu.make_async_copy(
            dq_v.at[:, kv * QC : (kv + 1) * QC], dq_out.at[:, kv * QC : (kv + 1) * QC], osem.at[7 + kv]
        )
        copy.start()
        outs.append(copy)

    b_y[ypos, nb + 2 * KV :] = jnp.zeros((16 - nb - 2 * KV, D), F32)
    for d in range(1, 2 * NY):
        remote(b_y.at[ypos], b_y.at[ypos], bs1, br1, yydev(d)).start()
    for src, dst, i in ((dks_v, dks_out, 1), (dvs_v, dvs_out, 2)):
        copy = pltpu.make_async_copy(src, dst, osem.at[i])
        copy.start()
        outs.append(copy)
    reduce_y(KV - 1)
    await_recv(b_y.at[0 : 2 * NY - 1], br1)
    acc = b_y[0]
    for i in range(1, 2 * NY):
        acc = acc + b_y[i]
    b_z[pl.ds(zpos, 1)] = acc[None]
    for d in range(1, 2 * NZ):
        remote(b_z.at[zpos], b_z.at[zpos], bs2, br2, zzdev(d)).start()
    reduce_z(KV - 1)
    for src, dst, i in ((dpk_v, dpk_out, 3), (dpv_v, dpv_out, 4)):
        copy = pltpu.make_async_copy(src, dst, osem.at[i])
        copy.start()
        outs.append(copy)

    for kind in (0, 1):
        await_send(q_st.at[0 : KV * RATIO * (NX - 1) * TOK], xs.at[kind])
    await_send(q_st.at[0 : 2 * KV * (NX - 1) * TOK], kvs)
    for kv in range(KV):
        await_send(kv_all.at[kv, 0 : (NZ - 1) * PIECE], gzs.at[kv])
        await_send(kv_all.at[kv, 0 : NZ * (NY - 1) * PIECE], gys.at[kv])
        await_send(kv_all.at[kv, 0:HALF], gss.at[kv])
        rsib(kv).wait_send()
        await_send(kv_all.at[kv, 0 : NZ * (NY - 1) * PIECE], r1s.at[kv])
        await_send(rs_z.at[kv], r2s.at[kv])
    await_send(b_y.at[0 : 2 * NY - 1], bs1)

    await_recv(b_z.at[0 : 2 * NZ - 1], br2)
    acc = b_z[0]
    for i in range(1, 2 * NZ):
        acc = acc + b_z[i]
    qb_v[...] = acc[:nb]
    for kv in range(KV):
        kvb_v[0:1, kv * D : (kv + 1) * D] = acc[nb + kv : nb + kv + 1]
        kvb_v[1:2, kv * D : (kv + 1) * D] = acc[nb + KV + kv : nb + KV + kv + 1]
    for src, dst, i in ((qb_v, qb_out, 5), (kvb_v, kvb_out, 6)):
        copy = pltpu.make_async_copy(src, dst, osem.at[i])
        copy.start()
        outs.append(copy)
    await_send(b_z.at[0 : 2 * NZ - 1], bs2)
    for copy in outs:
        copy.wait()


def finish(*refs):
    n = (len(refs) - 2) // 3
    sem_in, sem_out = refs[-2:]
    first, second = [], []
    for i in range(n):
        src, dst, held = refs[i], refs[n + i], refs[2 * n + i]
        parts = 4 if i == 0 else 1
        step = src.shape[0] // parts
        for j in range(parts):
            rows = pl.ds(j * step, step)
            k = len(first)
            first.append(pltpu.make_async_copy(src.at[rows], held.at[rows], sem_in.at[k]))
            second.append(pltpu.make_async_copy(held.at[rows], dst.at[rows], sem_out.at[k]))
    for copy in first:
        copy.start()
    for a, b in zip(first, second):
        a.wait()
        b.start()
    for copy in second:
        copy.wait()


def local(queries, suffix_keys, suffix_values, d_out, prefix_keys, prefix_values, advantages, lengths):
    sds = jax.ShapeDtypeStruct
    dma = pltpu.SemaphoreType.DMA
    hbm = pl.BlockSpec(memory_space=pl.ANY)
    smem = pl.BlockSpec(memory_space=pltpu.SMEM)
    nb = KV * RATIO
    vm = pltpu.VMEM
    shapes = (
        sds((RESP, KV * QC), BF16),
        sds((RESP, KV * D), BF16),
        sds((RESP, KV * D), BF16),
        sds((PIECE, KV * D), BF16),
        sds((PIECE, KV * D), BF16),
        sds((nb, D), F32),
        sds((2, KV * D), F32),
    )
    out = pl.pallas_call(
        kernel,
        out_shape=shapes,
        in_specs=[hbm] * 6 + [smem] * 2,
        out_specs=(hbm,) * 7,
        scratch_shapes=[
            vm((KV * QT, D), BF16), vm((KV * QT, D), BF16), vm((KV * QT, D), BF16),
            vm((KV, KEYS, 2 * D), BF16),
            vm((D, KEYS), BF16),
            vm((KEYS, RESP), F32), vm((KEYS, RESP), F32),
            vm((KEYS, QT), BF16), vm((KEYS, QT), BF16),
            vm((RESP, KV * QC), BF16), vm((RESP, KV * D), BF16), vm((RESP, KV * D), BF16),
            vm((KV, HALF, 2 * D), BF16), vm((KV, HALF, 2 * D), BF16), vm((HALF, 2 * D), F32),
            vm((KV, HALF, 2 * D), BF16), vm((KV, NZ, NY - 1, PIECE, 2 * D), BF16),
            vm((PIECE, 2 * D), F32), vm((KV, NZ - 1, PIECE, 2 * D), BF16),
            vm((KV, NZ - 1, PIECE, 2 * D), BF16), vm((PIECE, KV * D), BF16), vm((PIECE, KV * D), BF16),
            vm((2 * NY, 16, D), F32), vm((2 * NZ, 16, D), F32),
            vm((nb, D), F32), vm((2, KV * D), F32),
            dma((2,)), dma((2, nb)), dma, dma((KV,)), dma((KV,)),
            dma((KV,)), dma((KV, NZ - 1)), dma((KV,)), dma((KV, NZ)), dma((KV,)), dma((KV,)),
            dma((KV,)), dma((KV,)), dma((KV,)), dma((KV, NZ)), dma((KV,)), dma((KV,)),
            dma, dma, dma, dma,
            dma((9,)),
        ],
        compiler_params=pltpu.CompilerParams(
            collective_id=0, has_side_effects=True, vmem_limit_bytes=60 * 1024 * 1024
        ),
        name="grouped_attention_backward",
    )(
        queries[0, 0], suffix_keys[0, 0], suffix_values[0, 0], d_out[0, 0],
        prefix_keys[0], prefix_values[0], advantages, lengths,
    )
    out = pl.pallas_call(
        finish,
        out_shape=shapes,
        in_specs=[hbm] * 7,
        out_specs=(hbm,) * 7,
        scratch_shapes=[vm(s.shape, s.dtype) for s in shapes] + [dma((10,)), dma((10,))],
        compiler_params=pltpu.CompilerParams(vmem_limit_bytes=60 * 1024 * 1024),
        name="finish",
    )(*out)
    dq, dks, dvs, dpk, dpv, qb, kvb = out
    return (dq[None, None], dks[None, None], dvs[None, None], dpk[None], dpv[None], qb.reshape(-1), kvb)


def solution(mesh):
    in_specs = (
        P("dp", "group", "tensor", None),
        P("dp", "group", "tensor", None),
        P("dp", "group", "tensor", None),
        P("dp", "group", "tensor", None),
        P("dp", "group", "tensor"),
        P("dp", "group", "tensor"),
        P("dp", "group"),
        P("dp", "group"),
    )
    out_specs = (
        P("dp", "group", None, "tensor"),
        P("dp", "group", None, "tensor"),
        P("dp", "group", None, "tensor"),
        P("dp", "group", "tensor"),
        P("dp", "group", "tensor"),
        P("tensor"),
        P(None, "tensor"),
    )
    return jax.shard_map(local, mesh=mesh, in_specs=in_specs, out_specs=out_specs, check_vma=False)
```

```python
import math

import jax
import jax.numpy as jnp
from jax import lax
from jax.experimental import pallas as pl
from jax.experimental.pallas import tpu as pltpu
from jax.sharding import PartitionSpec as P

H = 40
KEY_VALUE_HEADS = 8
D = 128
RATIO = H // KEY_VALUE_HEADS
NX = 4
NY = 4
NZ = 4
KV = KEY_VALUE_HEADS // NX
TOK = 64
RESP = NX * TOK
QC = RATIO * D
PRE = 1024
KEYS = PRE + RESP
PIECE = PRE // (2 * NY * NZ)
YROWS = NZ * PIECE
HALF = NY * YROWS
QT = RATIO * RESP
SCALE = D ** -0.5
C2 = SCALE * math.log2(math.e)
MESH = pl.DeviceIdType.MESH
F32 = jnp.float32
BF16 = jnp.bfloat16


def nt(a, b):
    return lax.dot_general(a, b, (((1,), (1,)), ((), ())), preferred_element_type=F32)


def nn(a, b):
    return lax.dot_general(a, b, (((1,), (0,)), ((), ())), preferred_element_type=F32)


def fold(a, op):
    return op(a.reshape(a.shape[0] // 8, 8, a.shape[1]), axis=0)


def kernel(
    q_in, ks_in, vs_in, do_in, pk_in, pv_in, adv_ref, len_ref,
    dq_out, dks_out, dvs_out, dpk_out, dpv_out, qb_out, kvb_out,
    q_st, do_st, c_st, kv_all, k_t, s_buf, dp_buf, p_a, ds_a, p_b, ds_b, acc_kv,
    rs_snd, rs_sib, rs_snd2, rs_y, b_y, b_z,
    xs, xr, kvs, kvr, gl, gzs, gzr, gys, gyr, gss, gsr,
    r0s, r0r, r1s, r1r, bs1, br1, bs2, br2, spare,
):
    g = lax.axis_index("group")
    x = lax.axis_index("tensor")
    dp = lax.axis_index("dp")
    core = lax.rem(g, 2)
    zh = lax.rem(g // 2, NZ)
    y = g // (2 * NZ)
    sib = {"group": g + 1 - 2 * core}

    def xdev(d):
        return {"tensor": lax.rem(x + d, NX)}

    def ydev(d):
        return {"group": lax.rem(y + d, NY) * (2 * NZ) + zh * 2 + core}

    def zdev(d):
        return {"group": y * (2 * NZ) + lax.rem(zh + d, NZ) * 2 + core}

    ypos = y * 2 + core
    zpos = zh * 2 + dp

    def yydev(d):
        p = lax.rem(ypos + d, 2 * NY)
        return {"group": (p // 2) * (2 * NZ) + zh * 2 + lax.rem(p, 2)}

    def zzdev(d):
        p = lax.rem(zpos + d, 2 * NZ)
        return {"group": y * (2 * NZ) + (p // 2) * 2 + core, "dp": lax.rem(p, 2)}

    def remote(src, dst, ss, rs, dev):
        return pltpu.make_async_remote_copy(
            src_ref=src, dst_ref=dst, send_sem=ss, recv_sem=rs, device_id=dev, device_id_type=MESH
        )

    def await_recv(ref, sem):
        remote(ref, ref, spare, sem, sib).wait_recv()

    def await_send(ref, sem):
        remote(ref, ref, sem, spare, sib).wait_send()

    barrier = pltpu.get_barrier_semaphore()
    peers = [xdev(d) for d in range(1, NX)] + [yydev(d) for d in range(1, 2 * NY)]
    peers += [zzdev(d) for d in range(1, 2 * NZ)]
    for dev in peers:
        pl.semaphore_signal(barrier, inc=1, device_id=dev, device_id_type=MESH)

    def xsrc(kind, owner, r):
        return (q_in, do_in)[kind].at[:, pl.ds(pl.multiple_of((owner * KV * RATIO + r) * D, D), D)]

    def xdst(kind, source, r):
        return (q_st, do_st)[kind].at[pl.ds(pl.multiple_of(r * RESP + source * TOK, TOK), TOK)]

    def ksrc(kind, owner, kv):
        return (ks_in, vs_in)[kind].at[:, pl.ds(pl.multiple_of((owner * KV + kv) * D, D), D)]

    def kdst(kind, source, kv):
        return kv_all.at[kv, pl.ds(pl.multiple_of(PRE + source * TOK, TOK), TOK), kind * D : (kind + 1) * D]

    def start_head(r):
        for kind in (0, 1):
            for d in (2, 1, 3):
                src = xsrc(kind, lax.rem(x + d, NX), r)
                remote(src, xdst(kind, x, r), xs.at[kind], xr.at[kind, r], xdev(d)).start()

    def start_keys(kv):
        for kind in (0, 1):
            for d in (2, 1, 3):
                src = ksrc(kind, lax.rem(x + d, NX), kv)
                remote(src, kdst(kind, x, kv), kvs, kvr.at[kv], xdev(d)).start()

    def prow(c, zz, yy, n=PIECE):
        return pl.ds(pl.multiple_of(c * HALF + zz * YROWS + yy * PIECE, PIECE), n)

    def from_z(e):
        return lax.rem(zh + NZ - e, NZ)

    def gather_z(kv):
        own = kv_all.at[kv, prow(core, zh, y)]
        for d in (2, 1, 3):
            remote(own, own, gzs.at[kv], gzr.at[kv, d - 1], zdev(d)).start()

    def gather_y(kv, e):
        blk = kv_all.at[kv, prow(core, from_z(e), y)]
        if e > 0:
            await_recv(blk, gzr.at[kv, e - 1])
        for d in (2, 1, 3):
            remote(blk, blk, gys.at[kv], gyr.at[kv, e], ydev(d)).start()

    def gather_sib(kv, e):
        await_recv(kv_all.at[kv, 0 : (NY - 1) * PIECE], gyr.at[kv, e])
        blk = kv_all.at[kv, prow(core, from_z(e), 0, YROWS)]
        remote(blk, blk, gss.at[kv], gsr.at[kv], sib).start()

    def gather_done(kv):
        await_recv(kv_all.at[kv, 0:HALF], gsr.at[kv])

    for kv in range(KV):
        for kind in (0, 1):
            dst = kv_all.at[kv, prow(core, zh, y), kind * D : (kind + 1) * D]
            pltpu.make_async_copy((pk_in, pv_in)[kind].at[:, kv * D : (kv + 1) * D], dst, gl.at[kv]).start()
    for kv in range(KV):
        await_recv(kv_all.at[kv, 0:PIECE], gl.at[kv])

    pl.semaphore_wait(barrier, len(peers))

    gather_z(0)
    gather_y(0, 0)
    start_head(0)
    start_keys(0)
    gather_z(1)
    gather_y(1, 0)
    for h in range(1, RATIO):
        start_head(h)
    for r in range(KV * RATIO):
        for kind in (0, 1):
            pltpu.make_async_copy(xsrc(kind, x, r), xdst(kind, x, r), xr.at[kind, r]).start()
    for kv in range(KV):
        for kind in (0, 1):
            pltpu.make_async_copy(ksrc(kind, x, kv), kdst(kind, x, kv), kvr.at[kv]).start()
    order = (1, 3, 2)
    for e in order:
        gather_y(0, e)
    start_keys(1)
    start_head(RATIO)
    for e in order:
        gather_y(1, e)
    start_head(RATIO + 1)
    for e in (0,) + order:
        gather_sib(0, e)
    for h in range(2, RATIO):
        start_head(RATIO + h)
    acc_kv[...] = jnp.zeros_like(acc_kv)

    length = len_ref[0, 0]
    tok = lax.broadcasted_iota(jnp.int32, (RESP, 1), 0)
    weight = jnp.full((RESP, 1), adv_ref[0, 0], F32) / jnp.full((RESP, 1), length.astype(F32), F32)
    factor = jnp.where(tok < length, weight, 0.0)

    def seen():
        s = lax.broadcasted_iota(jnp.int32, (RESP, RESP), 0)
        t = lax.broadcasted_iota(jnp.int32, (RESP, RESP), 1)
        return (s <= t) & (s < length)

    nblk = KEYS // RESP

    def blk(b):
        return slice(b * RESP, (b + 1) * RESP)

    def qrows(r):
        return pl.ds(pl.multiple_of(r * RESP, RESP), RESP)

    def arrive(r):
        for kind in (0, 1):
            await_recv((q_st, do_st)[kind].at[qrows(r)], xr.at[kind, r])

    def query_grad(o, ds_old):
        dqh = (nn(k_t[o // RATIO], ds_old[...]) * SCALE).T
        dq_out[:, pl.ds(pl.multiple_of(o * D, D), D)] = dqh.astype(BF16)
        b_y[ypos, pl.ds(o, 1)] = jnp.sum(dqh, axis=0, keepdims=True)

    def step(r, p_new, ds_new, p_old, ds_old):
        arrive(r)
        kv = r // RATIO
        qh = q_st[qrows(r)]
        ch = (do_st[qrows(r)].astype(F32) * factor).astype(BF16)
        c_st[qrows(r)] = ch
        o = r - 1
        top = total = accum = None
        if p_old is not None:
            okv = o // RATIO
            qo = q_st[qrows(o)]
            co = c_st[qrows(o)]

        for b in range(nblk):
            s = nt(kv_all[kv, blk(b), :D], qh)
            if b == nblk - 1:
                s = jnp.where(seen(), s, -1e30)
            s_buf[blk(b)] = s
            m = fold(s, jnp.max)
            top = m if top is None else jnp.maximum(top, m)
        top = jnp.max(top, axis=0, keepdims=True) * C2
        if p_old is not None:
            query_grad(o, ds_old)
        for b in range(nblk):
            if p_old is not None:
                acc_kv[okv, blk(b), D:] += nn(p_old[blk(b)], co)
            dpr = nt(kv_all[kv, blk(b), D:], ch)
            e = jnp.exp2(s_buf[blk(b)] * C2 - top)
            s_buf[blk(b)] = e
            dp_buf[blk(b)] = dpr
            t1 = fold(e, jnp.sum)
            t2 = fold(e * dpr, jnp.sum)
            total = t1 if total is None else total + t1
            accum = t2 if accum is None else accum + t2
        total = jnp.sum(total, axis=0, keepdims=True)
        accum = jnp.sum(accum, axis=0, keepdims=True)
        inv = 1.0 / total
        delta = accum * inv
        for b in range(nblk):
            if p_old is not None:
                acc_kv[okv, blk(b), :D] += nn(ds_old[blk(b)], qo)
            p = s_buf[blk(b)] * inv
            p_new[blk(b)] = p.astype(BF16)
            ds_new[blk(b)] = (p * (dp_buf[blk(b)] - delta)).astype(BF16)

    def rsib(kv):
        return remote(rs_snd.at[kv], rs_sib.at[kv], r0s.at[kv], r0r.at[kv], sib)

    def hops(e, d):
        return 2 * min(e, NZ - e) + min(d, NY - d)

    owners = [(e, d) for e in range(NZ) for d in range(NY) if (e, d) != (0, 0)]
    owners.sort(key=lambda p: -hops(*p))

    def odev(e, d):
        return {"group": lax.rem(y + d, NY) * (2 * NZ) + lax.rem(zh + e, NZ) * 2 + core}

    def zyrows(e, d):
        zz, yy = lax.rem(zh + e, NZ), lax.rem(y + d, NY)
        return pl.ds(pl.multiple_of(zz * YROWS + yy * PIECE, PIECE), PIECE)

    lane = lax.broadcasted_iota(jnp.int32, (1, 2 * D), 1)
    scales = jnp.where(lane < D, SCALE, 1.0)

    def half(kv, c, rows=None):
        base = pl.multiple_of(c * HALF, HALF)
        rows = pl.ds(base, HALF) if rows is None else pl.ds(base + rows.start, rows.size)
        return acc_kv[kv, rows] * scales

    def own_rows(kv, rows):
        return half(kv, core, rows) + rs_sib[kv, rows].astype(F32)

    def reduce_send(kv):
        rsib(kv).wait_recv()
        rs_snd2[kv] = (half(kv, core) + rs_sib[kv].astype(F32)).astype(BF16)
        for i, (e, d) in enumerate(owners):
            remote(rs_snd2.at[kv, zyrows(e, d)], rs_y.at[kv, i], r1s.at[kv], r1r.at[kv], odev(e, d)).start()

    def reduce_done(kv):
        await_recv(rs_y.at[kv], r1r.at[kv])
        acc = own_rows(kv, zyrows(0, 0))
        for i in range(len(owners)):
            acc = acc + rs_y[kv, i].astype(F32)
        dpk_out[:, kv * D : (kv + 1) * D] = acc[:, :D].astype(BF16)
        dpv_out[:, kv * D : (kv + 1) * D] = acc[:, D:].astype(BF16)

    nb = KV * RATIO

    def send_half(kv):
        rs_snd[kv] = half(kv, 1 - core).astype(BF16)
        rsib(kv).start()

    def suffix(kv):
        lanes = slice(kv * D, (kv + 1) * D)
        dks = acc_kv[kv, PRE:, :D] * SCALE
        dvs = acc_kv[kv, PRE:, D:]
        dks_out[:, lanes] = dks.astype(BF16)
        dvs_out[:, lanes] = dvs.astype(BF16)
        b_y[ypos, nb + kv : nb + kv + 1] = jnp.sum(dks, axis=0, keepdims=True)
        b_y[ypos, nb + KV + kv : nb + KV + kv + 1] = jnp.sum(dvs, axis=0, keepdims=True)

    b_y[ypos] = jnp.zeros((16, D), F32)

    def ready(kv):
        gather_done(kv)
        await_recv(kv_all.at[kv, PRE:KEYS], kvr.at[kv])
        k_t[kv] = kv_all[kv, :, :D].T

    bufs_a, bufs_b = (p_a, ds_a), (p_b, ds_b)
    ready(0)
    step(0, *bufs_a, None, None)

    def pair(i, carry):
        @pl.when(i == 0)
        def _():
            for e in (0,) + order:
                gather_sib(1, e)

        @pl.when(i == 2)
        def _():
            ready(1)

        @pl.when(i == 3)
        def _():
            reduce_send(0)

        step(2 * i + 1, *bufs_b, *bufs_a)

        @pl.when(i == 2)
        def _():
            send_half(0)
            suffix(0)

        step(2 * i + 2, *bufs_a, *bufs_b)
        return carry

    lax.fori_loop(0, nb // 2 - 1, pair, 0)
    step(nb - 1, *bufs_b, *bufs_a)

    o = nb - 1
    qo = q_st[o * RESP : (o + 1) * RESP]
    co = c_st[o * RESP : (o + 1) * RESP]
    other = pl.ds(pl.multiple_of((1 - core) * HALF, HALF), HALF)
    mine = pl.ds(pl.multiple_of(core * HALF, HALF), HALF)
    rs_snd[1, :, :D] = ((acc_kv[1, other, :D] + nn(ds_b[other], qo)) * SCALE).astype(BF16)
    rs_snd[1, :, D:] = (acc_kv[1, other, D:] + nn(p_b[other], co)).astype(BF16)
    rsib(1).start()
    for rows in (mine, slice(PRE, KEYS)):
        acc_kv[1, rows, :D] += nn(ds_b[rows], qo)
        acc_kv[1, rows, D:] += nn(p_b[rows], co)
    query_grad(o, ds_b)
    suffix(1)

    for d in range(1, 2 * NY):
        remote(b_y.at[ypos], b_y.at[ypos], bs1, br1, yydev(d)).start()
    reduce_send(1)
    reduce_done(0)
    await_recv(b_y.at[0 : 2 * NY - 1], br1)
    acc = b_y[0]
    for i in range(1, 2 * NY):
        acc = acc + b_y[i]
    b_z[pl.ds(zpos, 1)] = acc[None]
    for d in range(1, 2 * NZ):
        remote(b_z.at[zpos], b_z.at[zpos], bs2, br2, zzdev(d)).start()

    for kind in (0, 1):
        await_send(q_st.at[0 : KV * RATIO * (NX - 1) * TOK], xs.at[kind])
    await_send(q_st.at[0 : 2 * KV * (NX - 1) * TOK], kvs)
    for kv in range(KV):
        await_send(kv_all.at[kv, 0 : (NZ - 1) * PIECE], gzs.at[kv])
        await_send(kv_all.at[kv, 0 : NZ * (NY - 1) * PIECE], gys.at[kv])
        await_send(kv_all.at[kv, 0:HALF], gss.at[kv])
        rsib(kv).wait_send()
    await_send(b_y.at[0 : 2 * NY - 1], bs1)

    await_recv(b_z.at[0 : 2 * NZ - 1], br2)
    acc = b_z[0]
    for i in range(1, 2 * NZ):
        acc = acc + b_z[i]
    qb_out[...] = acc[:nb]
    for kv in range(KV):
        kvb_out[0:1, kv * D : (kv + 1) * D] = acc[nb + kv : nb + kv + 1]
        kvb_out[1:2, kv * D : (kv + 1) * D] = acc[nb + KV + kv : nb + KV + kv + 1]
    reduce_done(1)
    for kv in range(KV):
        await_send(rs_y.at[kv], r1s.at[kv])
    await_send(b_z.at[0 : 2 * NZ - 1], bs2)


def finish(*refs):
    n = (len(refs) - 1) // 2
    sem = refs[-1]
    copies = []
    for i in range(n):
        src, dst = refs[i], refs[n + i]
        parts = 4 if i == 0 else 1
        rows = src.shape[0] // parts
        for j in range(parts):
            part = pl.ds(j * rows, rows)
            copies.append(pltpu.make_async_copy(src.at[part], dst.at[part], sem.at[len(copies)]))
    for copy in copies:
        copy.start()
    for copy in copies:
        copy.wait()


def local(queries, suffix_keys, suffix_values, d_out, prefix_keys, prefix_values, advantages, lengths):
    sds = jax.ShapeDtypeStruct
    dma = pltpu.SemaphoreType.DMA
    hbm = pl.BlockSpec(memory_space=pl.ANY)
    smem = pl.BlockSpec(memory_space=pltpu.SMEM)
    nb = KV * RATIO
    vm = pltpu.VMEM
    shapes = (
        sds((RESP, KV * QC), BF16),
        sds((RESP, KV * D), BF16),
        sds((RESP, KV * D), BF16),
        sds((PIECE, KV * D), BF16),
        sds((PIECE, KV * D), BF16),
        sds((nb, D), F32),
        sds((2, KV * D), F32),
    )
    out = pl.pallas_call(
        kernel,
        out_shape=tuple(vm(s.shape, s.dtype) for s in shapes),
        in_specs=[hbm] * 6 + [smem] * 2,
        out_specs=(pl.BlockSpec(memory_space=vm),) * 7,
        scratch_shapes=[
            vm((KV * QT, D), BF16), vm((KV * QT, D), BF16), vm((KV * QT, D), BF16),
            vm((KV, KEYS, 2 * D), BF16),
            vm((KV, D, KEYS), BF16),
            vm((KEYS, RESP), F32), vm((KEYS, RESP), F32),
            vm((KEYS, RESP), BF16), vm((KEYS, RESP), BF16), vm((KEYS, RESP), BF16), vm((KEYS, RESP), BF16),
            vm((KV, KEYS, 2 * D), F32),
            vm((KV, HALF, 2 * D), BF16), vm((KV, HALF, 2 * D), BF16),
            vm((KV, HALF, 2 * D), BF16), vm((KV, NY * NZ - 1, PIECE, 2 * D), BF16),
            vm((2 * NY, 16, D), F32), vm((2 * NZ, 16, D), F32),
            dma((2,)), dma((2, nb)), dma, dma((KV,)), dma((KV,)),
            dma((KV,)), dma((KV, NZ - 1)), dma((KV,)), dma((KV, NZ)), dma((KV,)), dma((KV,)),
            dma((KV,)), dma((KV,)), dma((KV,)), dma((KV,)),
            dma, dma, dma, dma, dma,
        ],
        compiler_params=pltpu.CompilerParams(
            collective_id=0, has_side_effects=True, vmem_limit_bytes=60 * 1024 * 1024
        ),
        name="grouped_attention_backward",
    )(
        queries[0, 0], suffix_keys[0, 0], suffix_values[0, 0], d_out[0, 0],
        prefix_keys[0], prefix_values[0], advantages, lengths,
    )
    out = pl.pallas_call(
        finish,
        out_shape=shapes,
        in_specs=[hbm] * 7,
        out_specs=(hbm,) * 7,
        scratch_shapes=[dma((10,))],
        compiler_params=pltpu.CompilerParams(vmem_limit_bytes=4 * 1024 * 1024),
        name="finish",
    )(*out)
    dq, dks, dvs, dpk, dpv, qb, kvb = out
    return (dq[None, None], dks[None, None], dvs[None, None], dpk[None], dpv[None], qb.reshape(-1), kvb)


def solution(mesh):
    in_specs = (
        P("dp", "group", "tensor", None),
        P("dp", "group", "tensor", None),
        P("dp", "group", "tensor", None),
        P("dp", "group", "tensor", None),
        P("dp", "group", "tensor"),
        P("dp", "group", "tensor"),
        P("dp", "group"),
        P("dp", "group"),
    )
    out_specs = (
        P("dp", "group", None, "tensor"),
        P("dp", "group", None, "tensor"),
        P("dp", "group", None, "tensor"),
        P("dp", "group", "tensor"),
        P("dp", "group", "tensor"),
        P("tensor"),
        P(None, "tensor"),
    )
    return jax.shard_map(local, mesh=mesh, in_specs=in_specs, out_specs=out_specs, check_vma=False)
```

```python
import math

import jax
import jax.numpy as jnp
from jax import lax
from jax.experimental import pallas as pl
from jax.experimental.pallas import tpu as pltpu
from jax.sharding import PartitionSpec as P

H = 40
KEY_VALUE_HEADS = 8
D = 128
RATIO = H // KEY_VALUE_HEADS
NX = 4
NY = 4
NZ = 4
KV = KEY_VALUE_HEADS // NX
TOK = 64
RESP = NX * TOK
QC = RATIO * D
PRE = 1024
KEYS = PRE + RESP
PIECE = PRE // (2 * NY * NZ)
YROWS = NZ * PIECE
HALF = NY * YROWS
QT = RATIO * RESP
SCALE = D ** -0.5
C2 = SCALE * math.log2(math.e)
MESH = pl.DeviceIdType.MESH
F32 = jnp.float32
BF16 = jnp.bfloat16


def nt(a, b):
    return lax.dot_general(a, b, (((1,), (1,)), ((), ())), preferred_element_type=F32)


def nn(a, b):
    return lax.dot_general(a, b, (((1,), (0,)), ((), ())), preferred_element_type=F32)


def fold(a, op):
    return op(a.reshape(a.shape[0] // 8, 8, a.shape[1]), axis=0)


def kernel(
    q_in, ks_in, vs_in, do_in, pk_in, pv_in, adv_ref, len_ref,
    dq_out, dks_out, dvs_out, dpk_out, dpv_out, qb_out, kvb_out,
    q_st, do_st, c_st, kv_all, k_t, s_buf, dp_buf, p_a, ds_a, p_b, ds_b, acc_kv,
    rs_snd, rs_sib, rs_snd2, rs_y, b_y, b_z,
    xs, xr, kvs, kvr, gl, gzs, gzr, gys, gyr, gss, gsr,
    r0s, r0r, r1s, r1r, bs1, br1, bs2, br2, spare,
):
    g = lax.axis_index("group")
    x = lax.axis_index("tensor")
    dp = lax.axis_index("dp")
    core = lax.rem(g, 2)
    zh = lax.rem(g // 2, NZ)
    y = g // (2 * NZ)
    sib = {"group": g + 1 - 2 * core}

    def xdev(d):
        return {"tensor": lax.rem(x + d, NX)}

    def ydev(d):
        return {"group": lax.rem(y + d, NY) * (2 * NZ) + zh * 2 + core}

    def zdev(d):
        return {"group": y * (2 * NZ) + lax.rem(zh + d, NZ) * 2 + core}

    ypos = y * 2 + core
    zpos = zh * 2 + dp

    def yydev(d):
        p = lax.rem(ypos + d, 2 * NY)
        return {"group": (p // 2) * (2 * NZ) + zh * 2 + lax.rem(p, 2)}

    def zzdev(d):
        p = lax.rem(zpos + d, 2 * NZ)
        return {"group": y * (2 * NZ) + (p // 2) * 2 + core, "dp": lax.rem(p, 2)}

    def remote(src, dst, ss, rs, dev):
        return pltpu.make_async_remote_copy(
            src_ref=src, dst_ref=dst, send_sem=ss, recv_sem=rs, device_id=dev, device_id_type=MESH
        )

    def await_recv(ref, sem):
        remote(ref, ref, spare, sem, sib).wait_recv()

    def await_send(ref, sem):
        remote(ref, ref, sem, spare, sib).wait_send()

    barrier = pltpu.get_barrier_semaphore()
    peers = [xdev(d) for d in range(1, NX)] + [yydev(d) for d in range(1, 2 * NY)]
    peers += [zzdev(d) for d in range(1, 2 * NZ)]
    for dev in peers:
        pl.semaphore_signal(barrier, inc=1, device_id=dev, device_id_type=MESH)

    def xsrc(kind, owner, r):
        return (q_in, do_in)[kind].at[:, pl.ds(pl.multiple_of((owner * KV * RATIO + r) * D, D), D)]

    def xdst(kind, source, r):
        return (q_st, do_st)[kind].at[pl.ds(pl.multiple_of(r * RESP + source * TOK, TOK), TOK)]

    def ksrc(kind, owner, kv):
        return (ks_in, vs_in)[kind].at[:, pl.ds(pl.multiple_of((owner * KV + kv) * D, D), D)]

    def kdst(kind, source, kv):
        return kv_all.at[kv, pl.ds(pl.multiple_of(PRE + source * TOK, TOK), TOK), kind * D : (kind + 1) * D]

    def start_head(r):
        for kind in (0, 1):
            for d in (2, 1, 3):
                src = xsrc(kind, lax.rem(x + d, NX), r)
                remote(src, xdst(kind, x, r), xs.at[kind], xr.at[kind, r], xdev(d)).start()

    def start_keys(kv):
        for kind in (0, 1):
            for d in (2, 1, 3):
                src = ksrc(kind, lax.rem(x + d, NX), kv)
                remote(src, kdst(kind, x, kv), kvs, kvr.at[kv], xdev(d)).start()

    def prow(c, zz, yy, n=PIECE):
        return pl.ds(pl.multiple_of(c * HALF + zz * YROWS + yy * PIECE, PIECE), n)

    def from_z(e):
        return lax.rem(zh + NZ - e, NZ)

    def gather_z(kv):
        own = kv_all.at[kv, prow(core, zh, y)]
        for d in (2, 1, 3):
            remote(own, own, gzs.at[kv], gzr.at[kv, d - 1], zdev(d)).start()

    def gather_y(kv, e):
        blk = kv_all.at[kv, prow(core, from_z(e), y)]
        if e > 0:
            await_recv(blk, gzr.at[kv, e - 1])
        for d in (2, 1, 3):
            remote(blk, blk, gys.at[kv], gyr.at[kv, e], ydev(d)).start()

    def gather_sib(kv, e):
        await_recv(kv_all.at[kv, 0 : (NY - 1) * PIECE], gyr.at[kv, e])
        blk = kv_all.at[kv, prow(core, from_z(e), 0, YROWS)]
        remote(blk, blk, gss.at[kv], gsr.at[kv], sib).start()

    def gather_done(kv):
        await_recv(kv_all.at[kv, 0:HALF], gsr.at[kv])

    for kv in range(KV):
        for kind in (0, 1):
            dst = kv_all.at[kv, prow(core, zh, y), kind * D : (kind + 1) * D]
            pltpu.make_async_copy((pk_in, pv_in)[kind].at[:, kv * D : (kv + 1) * D], dst, gl.at[kv]).start()
    for kv in range(KV):
        await_recv(kv_all.at[kv, 0:PIECE], gl.at[kv])

    pl.semaphore_wait(barrier, len(peers))

    gather_z(0)
    gather_y(0, 0)
    start_head(0)
    start_keys(0)
    gather_z(1)
    gather_y(1, 0)
    for h in range(1, RATIO):
        start_head(h)
    for r in range(KV * RATIO):
        for kind in (0, 1):
            pltpu.make_async_copy(xsrc(kind, x, r), xdst(kind, x, r), xr.at[kind, r]).start()
    for kv in range(KV):
        for kind in (0, 1):
            pltpu.make_async_copy(ksrc(kind, x, kv), kdst(kind, x, kv), kvr.at[kv]).start()
    order = (1, 3, 2)
    for e in order:
        gather_y(0, e)
    start_keys(1)
    start_head(RATIO)
    for e in order:
        gather_y(1, e)
    start_head(RATIO + 1)
    for e in (0,) + order:
        gather_sib(0, e)
    for h in range(2, RATIO):
        start_head(RATIO + h)
    acc_kv[...] = jnp.zeros_like(acc_kv)

    length = len_ref[0, 0]
    tok = lax.broadcasted_iota(jnp.int32, (RESP, 1), 0)
    weight = jnp.full((RESP, 1), adv_ref[0, 0], F32) / jnp.full((RESP, 1), length.astype(F32), F32)
    factor = jnp.where(tok < length, weight, 0.0)

    def seen():
        s = lax.broadcasted_iota(jnp.int32, (RESP, RESP), 0)
        t = lax.broadcasted_iota(jnp.int32, (RESP, RESP), 1)
        return (s <= t) & (s < length)

    nblk = KEYS // RESP

    def blk(b):
        return slice(b * RESP, (b + 1) * RESP)

    def qrows(r):
        return pl.ds(pl.multiple_of(r * RESP, RESP), RESP)

    def arrive(r):
        for kind in (0, 1):
            await_recv((q_st, do_st)[kind].at[qrows(r)], xr.at[kind, r])

    def query_grad(o, ds_old):
        dqh = (nn(k_t[o // RATIO], ds_old[...]) * SCALE).T
        dq_out[:, pl.ds(pl.multiple_of(o * D, D), D)] = dqh.astype(BF16)
        b_z[zpos, pl.ds(o, 1)] = jnp.sum(dqh, axis=0, keepdims=True)

    def step(r, p_new, ds_new, p_old, ds_old):
        arrive(r)
        kv = r // RATIO
        qh = q_st[qrows(r)]
        ch = (do_st[qrows(r)].astype(F32) * factor).astype(BF16)
        c_st[qrows(r)] = ch
        o = r - 1
        top = total = accum = None
        if p_old is not None:
            okv = o // RATIO
            qo = q_st[qrows(o)]
            co = c_st[qrows(o)]

        for b in range(nblk):
            s = nt(kv_all[kv, blk(b), :D], qh)
            if b == nblk - 1:
                s = jnp.where(seen(), s, -1e30)
            s_buf[blk(b)] = s
            m = fold(s, jnp.max)
            top = m if top is None else jnp.maximum(top, m)
        top = jnp.max(top, axis=0, keepdims=True) * C2
        if p_old is not None:
            query_grad(o, ds_old)
        for b in range(nblk):
            if p_old is not None:
                acc_kv[okv, blk(b), D:] += nn(p_old[blk(b)], co)
            dpr = nt(kv_all[kv, blk(b), D:], ch)
            e = jnp.exp2(s_buf[blk(b)] * C2 - top)
            s_buf[blk(b)] = e
            dp_buf[blk(b)] = dpr
            t1 = fold(e, jnp.sum)
            t2 = fold(e * dpr, jnp.sum)
            total = t1 if total is None else total + t1
            accum = t2 if accum is None else accum + t2
        total = jnp.sum(total, axis=0, keepdims=True)
        accum = jnp.sum(accum, axis=0, keepdims=True)
        inv = 1.0 / total
        delta = accum * inv
        for b in range(nblk):
            if p_old is not None:
                acc_kv[okv, blk(b), :D] += nn(ds_old[blk(b)], qo)
            p = s_buf[blk(b)] * inv
            p_new[blk(b)] = p.astype(BF16)
            ds_new[blk(b)] = (p * (dp_buf[blk(b)] - delta)).astype(BF16)

    far = (2, 1, 3, 0)

    def zrows(e):
        return pl.ds(pl.multiple_of(lax.rem(zh + e, NZ) * YROWS, YROWS), YROWS)

    def rsib(kv, e):
        rows = zrows(e)
        return remote(rs_snd.at[kv, rows], rs_sib.at[kv, rows], r0s.at[kv], r0r.at[kv, e], sib)

    def send_sib(kv):
        for e in far:
            rsib(kv, e).start()

    owners = [(e, d) for e in far for d in far if (e, d) != (0, 0)]

    def odev(e, d):
        return {"group": lax.rem(y + d, NY) * (2 * NZ) + lax.rem(zh + e, NZ) * 2 + core}

    def zyrows(e, d):
        zz, yy = lax.rem(zh + e, NZ), lax.rem(y + d, NY)
        return pl.ds(pl.multiple_of(zz * YROWS + yy * PIECE, PIECE), PIECE)

    lane = lax.broadcasted_iota(jnp.int32, (1, 2 * D), 1)
    scales = jnp.where(lane < D, SCALE, 1.0)

    def half(kv, c, rows=None):
        base = pl.multiple_of(c * HALF, HALF)
        rows = pl.ds(base, HALF) if rows is None else pl.ds(base + rows.start, rows.size)
        return acc_kv[kv, rows] * scales

    def own_rows(kv, rows):
        return half(kv, core, rows) + rs_sib[kv, rows].astype(F32)

    def reduce_send(kv):
        for e in far:
            rsib(kv, e).wait_recv()
            rs_snd2[kv, zrows(e)] = own_rows(kv, zrows(e)).astype(BF16)
            for i, (ee, d) in enumerate(owners):
                if ee == e:
                    src = rs_snd2.at[kv, zyrows(e, d)]
                    remote(src, rs_y.at[kv, i], r1s.at[kv], r1r.at[kv], odev(e, d)).start()

    def reduce_done(kv):
        await_recv(rs_y.at[kv], r1r.at[kv])
        acc = own_rows(kv, zyrows(0, 0))
        for i in range(len(owners)):
            acc = acc + rs_y[kv, i].astype(F32)
        dpk_out[:, kv * D : (kv + 1) * D] = acc[:, :D].astype(BF16)
        dpv_out[:, kv * D : (kv + 1) * D] = acc[:, D:].astype(BF16)

    nb = KV * RATIO

    def send_half(kv):
        rs_snd[kv] = half(kv, 1 - core).astype(BF16)
        send_sib(kv)

    def suffix(kv):
        lanes = slice(kv * D, (kv + 1) * D)
        dks = acc_kv[kv, PRE:, :D] * SCALE
        dvs = acc_kv[kv, PRE:, D:]
        dks_out[:, lanes] = dks.astype(BF16)
        dvs_out[:, lanes] = dvs.astype(BF16)
        b_z[zpos, nb + kv : nb + kv + 1] = jnp.sum(dks, axis=0, keepdims=True)
        b_z[zpos, nb + KV + kv : nb + KV + kv + 1] = jnp.sum(dvs, axis=0, keepdims=True)

    b_z[zpos] = jnp.zeros((16, D), F32)

    def ready(kv):
        gather_done(kv)
        await_recv(kv_all.at[kv, PRE:KEYS], kvr.at[kv])
        k_t[kv] = kv_all[kv, :, :D].T

    bufs_a, bufs_b = (p_a, ds_a), (p_b, ds_b)
    ready(0)
    step(0, *bufs_a, None, None)

    def pair(i, carry):
        @pl.when(i == 0)
        def _():
            for e in (0,) + order:
                gather_sib(1, e)

        @pl.when(i == 2)
        def _():
            ready(1)

        @pl.when(i == 3)
        def _():
            reduce_send(0)

        step(2 * i + 1, *bufs_b, *bufs_a)

        @pl.when(i == 2)
        def _():
            send_half(0)
            suffix(0)

        step(2 * i + 2, *bufs_a, *bufs_b)
        return carry

    lax.fori_loop(0, nb // 2 - 1, pair, 0)
    step(nb - 1, *bufs_b, *bufs_a)

    o = nb - 1
    qo = q_st[o * RESP : (o + 1) * RESP]
    co = c_st[o * RESP : (o + 1) * RESP]
    other = pl.ds(pl.multiple_of((1 - core) * HALF, HALF), HALF)
    mine = pl.ds(pl.multiple_of(core * HALF, HALF), HALF)
    rs_snd[1, :, :D] = ((acc_kv[1, other, :D] + nn(ds_b[other], qo)) * SCALE).astype(BF16)
    rs_snd[1, :, D:] = (acc_kv[1, other, D:] + nn(p_b[other], co)).astype(BF16)
    send_sib(1)
    for rows in (mine, slice(PRE, KEYS)):
        acc_kv[1, rows, :D] += nn(ds_b[rows], qo)
        acc_kv[1, rows, D:] += nn(p_b[rows], co)
    query_grad(o, ds_b)
    suffix(1)

    for d in (4, 3, 5, 2, 6, 1, 7):
        remote(b_z.at[zpos], b_z.at[zpos], bs2, br2, zzdev(d)).start()
    reduce_send(1)
    reduce_done(0)
    await_recv(b_z.at[0 : 2 * NZ - 1], br2)
    acc = b_z[0]
    for i in range(1, 2 * NZ):
        acc = acc + b_z[i]
    b_y[pl.ds(ypos, 1)] = acc[None]
    for d in range(1, 2 * NY):
        remote(b_y.at[ypos], b_y.at[ypos], bs1, br1, yydev(d)).start()

    for kind in (0, 1):
        await_send(q_st.at[0 : KV * RATIO * (NX - 1) * TOK], xs.at[kind])
    await_send(q_st.at[0 : 2 * KV * (NX - 1) * TOK], kvs)
    for kv in range(KV):
        await_send(kv_all.at[kv, 0 : (NZ - 1) * PIECE], gzs.at[kv])
        await_send(kv_all.at[kv, 0 : NZ * (NY - 1) * PIECE], gys.at[kv])
        await_send(kv_all.at[kv, 0:HALF], gss.at[kv])
        await_send(rs_snd.at[kv], r0s.at[kv])

    reduce_done(1)
    await_recv(b_y.at[0 : 2 * NY - 1], br1)
    acc = b_y[0]
    for i in range(1, 2 * NY):
        acc = acc + b_y[i]
    qb_out[...] = acc[:nb]
    for kv in range(KV):
        kvb_out[0:1, kv * D : (kv + 1) * D] = acc[nb + kv : nb + kv + 1]
        kvb_out[1:2, kv * D : (kv + 1) * D] = acc[nb + KV + kv : nb + KV + kv + 1]
    for kv in range(KV):
        await_send(rs_y.at[kv], r1s.at[kv])
    await_send(b_z.at[0 : 2 * NZ - 1], bs2)
    await_send(b_y.at[0 : 2 * NY - 1], bs1)


def finish(*refs):
    n = (len(refs) - 1) // 2
    sem = refs[-1]
    copies = []
    for i in range(n):
        src, dst = refs[i], refs[n + i]
        parts = 4 if i == 0 else 1
        rows = src.shape[0] // parts
        for j in range(parts):
            part = pl.ds(j * rows, rows)
            copies.append(pltpu.make_async_copy(src.at[part], dst.at[part], sem.at[len(copies)]))
    for copy in copies:
        copy.start()
    for copy in copies:
        copy.wait()


def local(queries, suffix_keys, suffix_values, d_out, prefix_keys, prefix_values, advantages, lengths):
    sds = jax.ShapeDtypeStruct
    dma = pltpu.SemaphoreType.DMA
    hbm = pl.BlockSpec(memory_space=pl.ANY)
    smem = pl.BlockSpec(memory_space=pltpu.SMEM)
    nb = KV * RATIO
    vm = pltpu.VMEM
    shapes = (
        sds((RESP, KV * QC), BF16),
        sds((RESP, KV * D), BF16),
        sds((RESP, KV * D), BF16),
        sds((PIECE, KV * D), BF16),
        sds((PIECE, KV * D), BF16),
        sds((nb, D), F32),
        sds((2, KV * D), F32),
    )
    out = pl.pallas_call(
        kernel,
        out_shape=tuple(vm(s.shape, s.dtype) for s in shapes),
        in_specs=[hbm] * 6 + [smem] * 2,
        out_specs=(pl.BlockSpec(memory_space=vm),) * 7,
        scratch_shapes=[
            vm((KV * QT, D), BF16), vm((KV * QT, D), BF16), vm((KV * QT, D), BF16),
            vm((KV, KEYS, 2 * D), BF16),
            vm((KV, D, KEYS), BF16),
            vm((KEYS, RESP), F32), vm((KEYS, RESP), F32),
            vm((KEYS, RESP), BF16), vm((KEYS, RESP), BF16), vm((KEYS, RESP), BF16), vm((KEYS, RESP), BF16),
            vm((KV, KEYS, 2 * D), F32),
            vm((KV, HALF, 2 * D), BF16), vm((KV, HALF, 2 * D), BF16),
            vm((KV, HALF, 2 * D), BF16), vm((KV, NY * NZ - 1, PIECE, 2 * D), BF16),
            vm((2 * NY, 16, D), F32), vm((2 * NZ, 16, D), F32),
            dma((2,)), dma((2, nb)), dma, dma((KV,)), dma((KV,)),
            dma((KV,)), dma((KV, NZ - 1)), dma((KV,)), dma((KV, NZ)), dma((KV,)), dma((KV,)),
            dma((KV,)), dma((KV, NZ)), dma((KV,)), dma((KV,)),
            dma, dma, dma, dma, dma,
        ],
        compiler_params=pltpu.CompilerParams(
            collective_id=0, has_side_effects=True, vmem_limit_bytes=60 * 1024 * 1024
        ),
        name="grouped_attention_backward",
    )(
        queries[0, 0], suffix_keys[0, 0], suffix_values[0, 0], d_out[0, 0],
        prefix_keys[0], prefix_values[0], advantages, lengths,
    )
    out = pl.pallas_call(
        finish,
        out_shape=shapes,
        in_specs=[hbm] * 7,
        out_specs=(hbm,) * 7,
        scratch_shapes=[dma((10,))],
        compiler_params=pltpu.CompilerParams(vmem_limit_bytes=4 * 1024 * 1024),
        name="finish",
    )(*out)
    dq, dks, dvs, dpk, dpv, qb, kvb = out
    return (dq[None, None], dks[None, None], dvs[None, None], dpk[None], dpv[None], qb.reshape(-1), kvb)


def solution(mesh):
    in_specs = (
        P("dp", "group", "tensor", None),
        P("dp", "group", "tensor", None),
        P("dp", "group", "tensor", None),
        P("dp", "group", "tensor", None),
        P("dp", "group", "tensor"),
        P("dp", "group", "tensor"),
        P("dp", "group"),
        P("dp", "group"),
    )
    out_specs = (
        P("dp", "group", None, "tensor"),
        P("dp", "group", None, "tensor"),
        P("dp", "group", None, "tensor"),
        P("dp", "group", "tensor"),
        P("dp", "group", "tensor"),
        P("tensor"),
        P(None, "tensor"),
    )
    return jax.shard_map(local, mesh=mesh, in_specs=in_specs, out_specs=out_specs, check_vma=False)
```

```python
import math

import jax
import jax.numpy as jnp
from jax import lax
from jax.experimental import pallas as pl
from jax.experimental.pallas import tpu as pltpu
from jax.sharding import PartitionSpec as P

H = 40
KEY_VALUE_HEADS = 8
D = 128
RATIO = H // KEY_VALUE_HEADS
NX = 4
NY = 4
NZ = 4
KV = KEY_VALUE_HEADS // NX
TOK = 64
RESP = NX * TOK
QC = RATIO * D
PRE = 1024
KEYS = PRE + RESP
PIECE = PRE // (2 * NY * NZ)
YROWS = NZ * PIECE
HALF = NY * YROWS
QT = RATIO * RESP
SCALE = D ** -0.5
C2 = SCALE * math.log2(math.e)
MESH = pl.DeviceIdType.MESH
F32 = jnp.float32
BF16 = jnp.bfloat16


def nt(a, b):
    return lax.dot_general(a, b, (((1,), (1,)), ((), ())), preferred_element_type=F32)


def nn(a, b):
    return lax.dot_general(a, b, (((1,), (0,)), ((), ())), preferred_element_type=F32)


def fold(a, op):
    return op(a.reshape(a.shape[0] // 8, 8, a.shape[1]), axis=0)


def kernel(
    q_in, ks_in, vs_in, do_in, pk_in, pv_in, adv_ref, len_ref,
    dq_out, dks_out, dvs_out, dpk_out, dpv_out, qb_out, kvb_out,
    q_st, do_st, c_st, kv_all, k_t, s_buf, dp_buf, p_a, ds_a, p_b, ds_b, acc_kv,
    rs_snd, rs_sib, rs_snd2, rs_y, b_y, b_z,
    xs, xr, kvs, kvr, gl, gzs, gzr, gys, gyr, gss, gsr,
    r0s, r0r, r1s, r1r, bs1, br1, bs2, br2, spare,
):
    g = lax.axis_index("group")
    x = lax.axis_index("tensor")
    dp = lax.axis_index("dp")
    core = lax.rem(g, 2)
    zh = lax.rem(g // 2, NZ)
    y = g // (2 * NZ)
    sib = {"group": g + 1 - 2 * core}

    def xdev(d):
        return {"tensor": lax.rem(x + d, NX)}

    def ydev(d):
        return {"group": lax.rem(y + d, NY) * (2 * NZ) + zh * 2 + core}

    def zdev(d):
        return {"group": y * (2 * NZ) + lax.rem(zh + d, NZ) * 2 + core}

    ypos = y * 2 + core
    zpos = zh * 2 + dp

    def yydev(d):
        p = lax.rem(ypos + d, 2 * NY)
        return {"group": (p // 2) * (2 * NZ) + zh * 2 + lax.rem(p, 2)}

    def zzdev(d):
        p = lax.rem(zpos + d, 2 * NZ)
        return {"group": y * (2 * NZ) + (p // 2) * 2 + core, "dp": lax.rem(p, 2)}

    def remote(src, dst, ss, rs, dev):
        return pltpu.make_async_remote_copy(
            src_ref=src, dst_ref=dst, send_sem=ss, recv_sem=rs, device_id=dev, device_id_type=MESH
        )

    def await_recv(ref, sem):
        remote(ref, ref, spare, sem, sib).wait_recv()

    def await_send(ref, sem):
        remote(ref, ref, sem, spare, sib).wait_send()

    barrier = pltpu.get_barrier_semaphore()
    peers = [zzdev(d) for d in (4, 3, 5, 2, 6, 1, 7)]
    peers += [yydev(d) for d in range(1, 2 * NY)] + [xdev(d) for d in (2, 1, 3)]
    for dev in peers:
        pl.semaphore_signal(barrier, inc=1, device_id=dev, device_id_type=MESH)

    def xsrc(kind, owner, r):
        return (q_in, do_in)[kind].at[:, pl.ds(pl.multiple_of((owner * KV * RATIO + r) * D, D), D)]

    def xdst(kind, source, r):
        return (q_st, do_st)[kind].at[pl.ds(pl.multiple_of(r * RESP + source * TOK, TOK), TOK)]

    def ksrc(kind, owner, kv):
        return (ks_in, vs_in)[kind].at[:, pl.ds(pl.multiple_of((owner * KV + kv) * D, D), D)]

    def kdst(kind, source, kv):
        return kv_all.at[kv, pl.ds(pl.multiple_of(PRE + source * TOK, TOK), TOK), kind * D : (kind + 1) * D]

    def start_head(r):
        for kind in (0, 1):
            for d in (2, 1, 3):
                src = xsrc(kind, lax.rem(x + d, NX), r)
                remote(src, xdst(kind, x, r), xs.at[kind], xr.at[kind, r], xdev(d)).start()

    def start_keys(kv):
        for kind in (0, 1):
            for d in (2, 1, 3):
                src = ksrc(kind, lax.rem(x + d, NX), kv)
                remote(src, kdst(kind, x, kv), kvs, kvr.at[kv], xdev(d)).start()

    def prow(c, zz, yy, n=PIECE):
        return pl.ds(pl.multiple_of(c * HALF + zz * YROWS + yy * PIECE, PIECE), n)

    def from_z(e):
        return lax.rem(zh + NZ - e, NZ)

    def gather_z(kv):
        own = kv_all.at[kv, prow(core, zh, y)]
        for d in (2, 1, 3):
            remote(own, own, gzs.at[kv], gzr.at[kv, d - 1], zdev(d)).start()

    def gather_y(kv, e):
        blk = kv_all.at[kv, prow(core, from_z(e), y)]
        if e > 0:
            await_recv(blk, gzr.at[kv, e - 1])
        for d in (2, 1, 3):
            remote(blk, blk, gys.at[kv], gyr.at[kv, e], ydev(d)).start()

    def gather_sib(kv, e):
        await_recv(kv_all.at[kv, 0 : (NY - 1) * PIECE], gyr.at[kv, e])
        blk = kv_all.at[kv, prow(core, from_z(e), 0, YROWS)]
        remote(blk, blk, gss.at[kv], gsr.at[kv], sib).start()

    def gather_done(kv):
        await_recv(kv_all.at[kv, 0:HALF], gsr.at[kv])

    for kv in range(KV):
        for kind in (0, 1):
            dst = kv_all.at[kv, prow(core, zh, y), kind * D : (kind + 1) * D]
            pltpu.make_async_copy((pk_in, pv_in)[kind].at[:, kv * D : (kv + 1) * D], dst, gl.at[kv]).start()
    for kv in range(KV):
        await_recv(kv_all.at[kv, 0:PIECE], gl.at[kv])

    pl.semaphore_wait(barrier, len(peers))

    gather_z(0)
    gather_y(0, 0)
    start_head(0)
    start_keys(0)
    gather_z(1)
    gather_y(1, 0)
    for h in range(1, RATIO):
        start_head(h)
    for r in range(KV * RATIO):
        for kind in (0, 1):
            pltpu.make_async_copy(xsrc(kind, x, r), xdst(kind, x, r), xr.at[kind, r]).start()
    for kv in range(KV):
        for kind in (0, 1):
            pltpu.make_async_copy(ksrc(kind, x, kv), kdst(kind, x, kv), kvr.at[kv]).start()
    order = (1, 3, 2)
    for e in order:
        gather_y(0, e)
    start_keys(1)
    start_head(RATIO)
    for e in order:
        gather_y(1, e)
    start_head(RATIO + 1)
    for e in (0,) + order:
        gather_sib(0, e)
    for h in range(2, RATIO):
        start_head(RATIO + h)
    acc_kv[...] = jnp.zeros_like(acc_kv)

    length = len_ref[0, 0]
    tok = lax.broadcasted_iota(jnp.int32, (RESP, 1), 0)
    weight = jnp.full((RESP, 1), adv_ref[0, 0], F32) / jnp.full((RESP, 1), length.astype(F32), F32)
    factor = jnp.where(tok < length, weight, 0.0)

    def seen():
        s = lax.broadcasted_iota(jnp.int32, (RESP, RESP), 0)
        t = lax.broadcasted_iota(jnp.int32, (RESP, RESP), 1)
        return (s <= t) & (s < length)

    nblk = KEYS // RESP

    def blk(b):
        return slice(b * RESP, (b + 1) * RESP)

    def qrows(r):
        return pl.ds(pl.multiple_of(r * RESP, RESP), RESP)

    def arrive(r):
        for kind in (0, 1):
            await_recv((q_st, do_st)[kind].at[qrows(r)], xr.at[kind, r])

    def query_grad(o, ds_old):
        dqh = (nn(k_t[o // RATIO], ds_old[...]) * SCALE).T
        dq_out[:, pl.ds(pl.multiple_of(o * D, D), D)] = dqh.astype(BF16)
        b_z[zpos, pl.ds(o, 1)] = jnp.sum(dqh, axis=0, keepdims=True)

    def step(r, p_new, ds_new, p_old, ds_old):
        arrive(r)
        kv = r // RATIO
        qh = q_st[qrows(r)]
        ch = (do_st[qrows(r)].astype(F32) * factor).astype(BF16)
        c_st[qrows(r)] = ch
        o = r - 1
        top = total = accum = None
        if p_old is not None:
            okv = o // RATIO
            qo = q_st[qrows(o)]
            co = c_st[qrows(o)]

        for b in range(nblk):
            s = nt(kv_all[kv, blk(b), :D], qh) * C2
            if b == nblk - 1:
                s = jnp.where(seen(), s, -1e30)
            s_buf[blk(b)] = s
            m = fold(s, jnp.max)
            top = m if top is None else jnp.maximum(top, m)
        top = jnp.max(top, axis=0, keepdims=True)
        if p_old is not None:
            query_grad(o, ds_old)
        for b in range(nblk):
            if p_old is not None:
                acc_kv[okv, blk(b), D:] += nn(p_old[blk(b)], co)
            dpr = nt(kv_all[kv, blk(b), D:], ch)
            e = jnp.exp2(s_buf[blk(b)] - top)
            s_buf[blk(b)] = e
            dp_buf[blk(b)] = dpr
            t1 = fold(e, jnp.sum)
            t2 = fold(e * dpr, jnp.sum)
            total = t1 if total is None else total + t1
            accum = t2 if accum is None else accum + t2
        total = jnp.sum(total, axis=0, keepdims=True)
        accum = jnp.sum(accum, axis=0, keepdims=True)
        inv = 1.0 / total
        delta = accum * inv
        for b in range(nblk):
            if p_old is not None:
                acc_kv[okv, blk(b), :D] += nn(ds_old[blk(b)], qo)
            p = s_buf[blk(b)] * inv
            p_new[blk(b)] = p.astype(BF16)
            ds_new[blk(b)] = (p * (dp_buf[blk(b)] - delta)).astype(BF16)

    far = (2, 1, 3, 0)

    def zrows(e):
        return pl.ds(pl.multiple_of(lax.rem(zh + e, NZ) * YROWS, YROWS), YROWS)

    def rsib(kv, e):
        rows = zrows(e)
        return remote(rs_snd.at[kv, rows], rs_sib.at[kv, rows], r0s.at[kv], r0r.at[kv, e], sib)

    def send_sib(kv):
        for e in far:
            rsib(kv, e).start()

    owners = [(e, d) for e in far for d in far if (e, d) != (0, 0)]

    def odev(e, d):
        return {"group": lax.rem(y + d, NY) * (2 * NZ) + lax.rem(zh + e, NZ) * 2 + core}

    def zyrows(e, d):
        zz, yy = lax.rem(zh + e, NZ), lax.rem(y + d, NY)
        return pl.ds(pl.multiple_of(zz * YROWS + yy * PIECE, PIECE), PIECE)

    lane = lax.broadcasted_iota(jnp.int32, (1, 2 * D), 1)
    scales = jnp.where(lane < D, SCALE, 1.0)

    def half(kv, c, rows=None):
        base = pl.multiple_of(c * HALF, HALF)
        rows = pl.ds(base, HALF) if rows is None else pl.ds(base + rows.start, rows.size)
        return acc_kv[kv, rows] * scales

    def own_rows(kv, rows):
        return half(kv, core, rows) + rs_sib[kv, rows].astype(F32)

    def reduce_send(kv):
        for e in far:
            rsib(kv, e).wait_recv()
            rs_snd2[kv, zrows(e)] = own_rows(kv, zrows(e)).astype(BF16)
            for i, (ee, d) in enumerate(owners):
                if ee == e:
                    src = rs_snd2.at[kv, zyrows(e, d)]
                    remote(src, rs_y.at[kv, i], r1s.at[kv], r1r.at[kv], odev(e, d)).start()

    def reduce_done(kv):
        await_recv(rs_y.at[kv], r1r.at[kv])
        acc = own_rows(kv, zyrows(0, 0))
        for i in range(len(owners)):
            acc = acc + rs_y[kv, i].astype(F32)
        dpk_out[:, kv * D : (kv + 1) * D] = acc[:, :D].astype(BF16)
        dpv_out[:, kv * D : (kv + 1) * D] = acc[:, D:].astype(BF16)

    nb = KV * RATIO

    def send_half(kv):
        rs_snd[kv] = half(kv, 1 - core).astype(BF16)
        send_sib(kv)

    def suffix(kv):
        lanes = slice(kv * D, (kv + 1) * D)
        dks = acc_kv[kv, PRE:, :D] * SCALE
        dvs = acc_kv[kv, PRE:, D:]
        dks_out[:, lanes] = dks.astype(BF16)
        dvs_out[:, lanes] = dvs.astype(BF16)
        b_z[zpos, nb + kv : nb + kv + 1] = jnp.sum(dks, axis=0, keepdims=True)
        b_z[zpos, nb + KV + kv : nb + KV + kv + 1] = jnp.sum(dvs, axis=0, keepdims=True)

    b_z[zpos] = jnp.zeros((16, D), F32)

    def turn(kv, c):
        rows = pl.ds(pl.multiple_of(c * HALF, HALF), HALF)
        k_t[kv, :, rows] = kv_all[kv, rows, :D].T

    def ready(kv):
        turn(kv, core)
        await_recv(kv_all.at[kv, PRE:KEYS], kvr.at[kv])
        k_t[kv, :, PRE:] = kv_all[kv, PRE:, :D].T
        gather_done(kv)
        turn(kv, 1 - core)

    bufs_a, bufs_b = (p_a, ds_a), (p_b, ds_b)
    ready(0)
    step(0, *bufs_a, None, None)

    def pair(i, carry):
        @pl.when(i == 0)
        def _():
            for e in (0,) + order:
                gather_sib(1, e)

        @pl.when(i == 2)
        def _():
            ready(1)

        @pl.when(i == 3)
        def _():
            reduce_send(0)

        step(2 * i + 1, *bufs_b, *bufs_a)

        @pl.when(i == 2)
        def _():
            send_half(0)
            suffix(0)

        step(2 * i + 2, *bufs_a, *bufs_b)
        return carry

    lax.fori_loop(0, nb // 2 - 1, pair, 0)
    step(nb - 1, *bufs_b, *bufs_a)

    o = nb - 1
    qo = q_st[o * RESP : (o + 1) * RESP]
    co = c_st[o * RESP : (o + 1) * RESP]
    other = pl.ds(pl.multiple_of((1 - core) * HALF, HALF), HALF)
    mine = pl.ds(pl.multiple_of(core * HALF, HALF), HALF)
    rs_snd[1, :, :D] = ((acc_kv[1, other, :D] + nn(ds_b[other], qo)) * SCALE).astype(BF16)
    rs_snd[1, :, D:] = (acc_kv[1, other, D:] + nn(p_b[other], co)).astype(BF16)
    send_sib(1)
    query_grad(o, ds_b)
    acc_kv[1, PRE:, :D] += nn(ds_b[PRE:], qo)
    acc_kv[1, PRE:, D:] += nn(p_b[PRE:], co)
    suffix(1)

    for d in (4, 3, 5, 2, 6, 1, 7):
        remote(b_z.at[zpos], b_z.at[zpos], bs2, br2, zzdev(d)).start()
    acc_kv[1, mine, :D] += nn(ds_b[mine], qo)
    acc_kv[1, mine, D:] += nn(p_b[mine], co)
    reduce_send(1)
    reduce_done(0)
    await_recv(b_z.at[0 : 2 * NZ - 1], br2)
    acc = b_z[0]
    for i in range(1, 2 * NZ):
        acc = acc + b_z[i]
    b_y[pl.ds(ypos, 1)] = acc[None]
    for d in range(1, 2 * NY):
        remote(b_y.at[ypos], b_y.at[ypos], bs1, br1, yydev(d)).start()

    for kind in (0, 1):
        await_send(q_st.at[0 : KV * RATIO * (NX - 1) * TOK], xs.at[kind])
    await_send(q_st.at[0 : 2 * KV * (NX - 1) * TOK], kvs)
    for kv in range(KV):
        await_send(kv_all.at[kv, 0 : (NZ - 1) * PIECE], gzs.at[kv])
        await_send(kv_all.at[kv, 0 : NZ * (NY - 1) * PIECE], gys.at[kv])
        await_send(kv_all.at[kv, 0:HALF], gss.at[kv])
        await_send(rs_snd.at[kv], r0s.at[kv])

    reduce_done(1)
    await_recv(b_y.at[0 : 2 * NY - 1], br1)
    acc = b_y[0]
    for i in range(1, 2 * NY):
        acc = acc + b_y[i]
    qb_out[...] = acc[:nb]
    for kv in range(KV):
        kvb_out[0:1, kv * D : (kv + 1) * D] = acc[nb + kv : nb + kv + 1]
        kvb_out[1:2, kv * D : (kv + 1) * D] = acc[nb + KV + kv : nb + KV + kv + 1]
    for kv in range(KV):
        await_send(rs_y.at[kv], r1s.at[kv])
    await_send(b_z.at[0 : 2 * NZ - 1], bs2)
    await_send(b_y.at[0 : 2 * NY - 1], bs1)


def finish(*refs):
    n = (len(refs) - 1) // 2
    sem = refs[-1]
    copies = []
    for i in range(n):
        src, dst = refs[i], refs[n + i]
        parts = 4 if i == 0 else 1
        rows = src.shape[0] // parts
        for j in range(parts):
            part = pl.ds(j * rows, rows)
            copies.append(pltpu.make_async_copy(src.at[part], dst.at[part], sem.at[len(copies)]))
    for copy in copies:
        copy.start()
    for copy in copies:
        copy.wait()


def local(queries, suffix_keys, suffix_values, d_out, prefix_keys, prefix_values, advantages, lengths):
    sds = jax.ShapeDtypeStruct
    dma = pltpu.SemaphoreType.DMA
    hbm = pl.BlockSpec(memory_space=pl.ANY)
    smem = pl.BlockSpec(memory_space=pltpu.SMEM)
    nb = KV * RATIO
    vm = pltpu.VMEM
    shapes = (
        sds((RESP, KV * QC), BF16),
        sds((RESP, KV * D), BF16),
        sds((RESP, KV * D), BF16),
        sds((PIECE, KV * D), BF16),
        sds((PIECE, KV * D), BF16),
        sds((nb, D), F32),
        sds((2, KV * D), F32),
    )
    out = pl.pallas_call(
        kernel,
        out_shape=tuple(vm(s.shape, s.dtype) for s in shapes),
        in_specs=[hbm] * 6 + [smem] * 2,
        out_specs=(pl.BlockSpec(memory_space=vm),) * 7,
        scratch_shapes=[
            vm((KV * QT, D), BF16), vm((KV * QT, D), BF16), vm((KV * QT, D), BF16),
            vm((KV, KEYS, 2 * D), BF16),
            vm((KV, D, KEYS), BF16),
            vm((KEYS, RESP), F32), vm((KEYS, RESP), F32),
            vm((KEYS, RESP), BF16), vm((KEYS, RESP), BF16), vm((KEYS, RESP), BF16), vm((KEYS, RESP), BF16),
            vm((KV, KEYS, 2 * D), F32),
            vm((KV, HALF, 2 * D), BF16), vm((KV, HALF, 2 * D), BF16),
            vm((KV, HALF, 2 * D), BF16), vm((KV, NY * NZ - 1, PIECE, 2 * D), BF16),
            vm((2 * NY, 16, D), F32), vm((2 * NZ, 16, D), F32),
            dma((2,)), dma((2, nb)), dma, dma((KV,)), dma((KV,)),
            dma((KV,)), dma((KV, NZ - 1)), dma((KV,)), dma((KV, NZ)), dma((KV,)), dma((KV,)),
            dma((KV,)), dma((KV, NZ)), dma((KV,)), dma((KV,)),
            dma, dma, dma, dma, dma,
        ],
        compiler_params=pltpu.CompilerParams(
            collective_id=0, has_side_effects=True, vmem_limit_bytes=60 * 1024 * 1024
        ),
        name="grouped_attention_backward",
    )(
        queries[0, 0], suffix_keys[0, 0], suffix_values[0, 0], d_out[0, 0],
        prefix_keys[0], prefix_values[0], advantages, lengths,
    )
    out = pl.pallas_call(
        finish,
        out_shape=shapes,
        in_specs=[hbm] * 7,
        out_specs=(hbm,) * 7,
        scratch_shapes=[dma((10,))],
        compiler_params=pltpu.CompilerParams(vmem_limit_bytes=4 * 1024 * 1024),
        name="finish",
    )(*out)
    dq, dks, dvs, dpk, dpv, qb, kvb = out
    return (dq[None, None], dks[None, None], dvs[None, None], dpk[None], dpv[None], qb.reshape(-1), kvb)


def solution(mesh):
    in_specs = (
        P("dp", "group", "tensor", None),
        P("dp", "group", "tensor", None),
        P("dp", "group", "tensor", None),
        P("dp", "group", "tensor", None),
        P("dp", "group", "tensor"),
        P("dp", "group", "tensor"),
        P("dp", "group"),
        P("dp", "group"),
    )
    out_specs = (
        P("dp", "group", None, "tensor"),
        P("dp", "group", None, "tensor"),
        P("dp", "group", None, "tensor"),
        P("dp", "group", "tensor"),
        P("dp", "group", "tensor"),
        P("tensor"),
        P(None, "tensor"),
    )
    return jax.shard_map(local, mesh=mesh, in_specs=in_specs, out_specs=out_specs, check_vma=False)
```

```python
import math

import jax
import jax.numpy as jnp
from jax import lax
from jax.experimental import pallas as pl
from jax.experimental.pallas import tpu as pltpu
from jax.sharding import PartitionSpec as P

H = 40
KEY_VALUE_HEADS = 8
D = 128
RATIO = H // KEY_VALUE_HEADS
NX = 4
NY = 4
NZ = 4
KV = KEY_VALUE_HEADS // NX
TOK = 64
RESP = NX * TOK
QC = RATIO * D
PRE = 1024
KEYS = PRE + RESP
PIECE = PRE // (2 * NY * NZ)
YROWS = NZ * PIECE
HALF = NY * YROWS
QT = RATIO * RESP
SCALE = D ** -0.5
C2 = SCALE * math.log2(math.e)
MESH = pl.DeviceIdType.MESH
F32 = jnp.float32
BF16 = jnp.bfloat16


def nt(a, b):
    return lax.dot_general(a, b, (((1,), (1,)), ((), ())), preferred_element_type=F32)


def nn(a, b):
    return lax.dot_general(a, b, (((1,), (0,)), ((), ())), preferred_element_type=F32)


def fold(a, op):
    return op(a.reshape(a.shape[0] // 8, 8, a.shape[1]), axis=0)


def kernel(
    q_in, ks_in, vs_in, do_in, pk_in, pv_in, adv_ref, len_ref,
    dq_out, dks_out, dvs_out, dpk_out, dpv_out, qb_out, kvb_out,
    q_st, do_st, c_st, kv_all, k_t, s_buf, dp_buf, p_a, ds_a, p_b, ds_b, acc_kv,
    rs_snd, rs_sib, rs_snd2, rs_y, b_y, b_z,
    xs, xr, kvs, kvr, gl, gzs, gzr, gys, gyr, gss, gsr,
    r0s, r0r, r1s, r1r, bs1, br1, bs2, br2, spare,
):
    g = lax.axis_index("group")
    x = lax.axis_index("tensor")
    dp = lax.axis_index("dp")
    core = lax.rem(g, 2)
    zh = lax.rem(g // 2, NZ)
    y = g // (2 * NZ)
    sib = {"group": g + 1 - 2 * core}

    def xdev(d):
        return {"tensor": lax.rem(x + d, NX)}

    def ydev(d):
        return {"group": lax.rem(y + d, NY) * (2 * NZ) + zh * 2 + core}

    def zdev(d):
        return {"group": y * (2 * NZ) + lax.rem(zh + d, NZ) * 2 + core}

    ypos = y * 2 + core
    zpos = zh * 2 + dp

    def yydev(d):
        p = lax.rem(ypos + d, 2 * NY)
        return {"group": (p // 2) * (2 * NZ) + zh * 2 + lax.rem(p, 2)}

    def zzdev(d):
        p = lax.rem(zpos + d, 2 * NZ)
        return {"group": y * (2 * NZ) + (p // 2) * 2 + core, "dp": lax.rem(p, 2)}

    def remote(src, dst, ss, rs, dev):
        return pltpu.make_async_remote_copy(
            src_ref=src, dst_ref=dst, send_sem=ss, recv_sem=rs, device_id=dev, device_id_type=MESH
        )

    def await_recv(ref, sem):
        remote(ref, ref, spare, sem, sib).wait_recv()

    def await_send(ref, sem):
        remote(ref, ref, sem, spare, sib).wait_send()

    barrier = pltpu.get_barrier_semaphore()
    peers = [xdev(d) for d in range(1, NX)] + [yydev(d) for d in range(1, 2 * NY)]
    peers += [zzdev(d) for d in range(1, 2 * NZ)]
    for dev in peers:
        pl.semaphore_signal(barrier, inc=1, device_id=dev, device_id_type=MESH)

    def xsrc(kind, owner, r):
        return (q_in, do_in)[kind].at[:, pl.ds(pl.multiple_of((owner * KV * RATIO + r) * D, D), D)]

    def xdst(kind, source, r):
        return (q_st, do_st)[kind].at[pl.ds(pl.multiple_of(r * RESP + source * TOK, TOK), TOK)]

    def ksrc(kind, owner, kv):
        return (ks_in, vs_in)[kind].at[:, pl.ds(pl.multiple_of((owner * KV + kv) * D, D), D)]

    def kdst(kind, source, kv):
        return kv_all.at[kv, pl.ds(pl.multiple_of(PRE + source * TOK, TOK), TOK), kind * D : (kind + 1) * D]

    def start_head(r):
        for kind in (0, 1):
            for d in (2, 1, 3):
                src = xsrc(kind, lax.rem(x + d, NX), r)
                remote(src, xdst(kind, x, r), xs.at[kind], xr.at[kind, r], xdev(d)).start()

    def start_keys(kv):
        for kind in (0, 1):
            for d in (2, 1, 3):
                src = ksrc(kind, lax.rem(x + d, NX), kv)
                remote(src, kdst(kind, x, kv), kvs, kvr.at[kv], xdev(d)).start()

    def prow(c, zz, yy, n=PIECE):
        return pl.ds(pl.multiple_of(c * HALF + zz * YROWS + yy * PIECE, PIECE), n)

    def from_z(e):
        return lax.rem(zh + NZ - e, NZ)

    def gather_z(kv):
        own = kv_all.at[kv, prow(core, zh, y)]
        for d in (2, 1, 3):
            remote(own, own, gzs.at[kv], gzr.at[kv, d - 1], zdev(d)).start()

    def gather_y(kv, e):
        blk = kv_all.at[kv, prow(core, from_z(e), y)]
        if e > 0:
            await_recv(blk, gzr.at[kv, e - 1])
        for d in (2, 1, 3):
            remote(blk, blk, gys.at[kv], gyr.at[kv, e], ydev(d)).start()

    def gather_sib(kv, e):
        await_recv(kv_all.at[kv, 0 : (NY - 1) * PIECE], gyr.at[kv, e])
        blk = kv_all.at[kv, prow(core, from_z(e), 0, YROWS)]
        remote(blk, blk, gss.at[kv], gsr.at[kv], sib).start()

    def gather_done(kv):
        await_recv(kv_all.at[kv, 0:HALF], gsr.at[kv])

    for kv in range(KV):
        for kind in (0, 1):
            dst = kv_all.at[kv, prow(core, zh, y), kind * D : (kind + 1) * D]
            pltpu.make_async_copy((pk_in, pv_in)[kind].at[:, kv * D : (kv + 1) * D], dst, gl.at[kv]).start()
    for kv in range(KV):
        await_recv(kv_all.at[kv, 0:PIECE], gl.at[kv])

    pl.semaphore_wait(barrier, len(peers))

    gather_z(0)
    gather_y(0, 0)
    start_head(0)
    start_keys(0)
    gather_z(1)
    gather_y(1, 0)
    for h in range(1, RATIO):
        start_head(h)
    for r in range(KV * RATIO):
        for kind in (0, 1):
            pltpu.make_async_copy(xsrc(kind, x, r), xdst(kind, x, r), xr.at[kind, r]).start()
    for kv in range(KV):
        for kind in (0, 1):
            pltpu.make_async_copy(ksrc(kind, x, kv), kdst(kind, x, kv), kvr.at[kv]).start()
    order = (1, 3, 2)
    for e in order:
        gather_y(0, e)
    start_keys(1)
    start_head(RATIO)
    for e in order:
        gather_y(1, e)
    start_head(RATIO + 1)
    for e in (0,) + order:
        gather_sib(0, e)
    for h in range(2, RATIO):
        start_head(RATIO + h)
    acc_kv[...] = jnp.zeros_like(acc_kv)

    length = len_ref[0, 0]
    tok = lax.broadcasted_iota(jnp.int32, (RESP, 1), 0)
    weight = jnp.full((RESP, 1), adv_ref[0, 0], F32) / jnp.full((RESP, 1), length.astype(F32), F32)
    factor = jnp.where(tok < length, weight, 0.0)

    def seen():
        s = lax.broadcasted_iota(jnp.int32, (RESP, RESP), 0)
        t = lax.broadcasted_iota(jnp.int32, (RESP, RESP), 1)
        return (s <= t) & (s < length)

    nblk = KEYS // RESP

    def blk(b):
        return slice(b * RESP, (b + 1) * RESP)

    def qrows(r):
        return pl.ds(pl.multiple_of(r * RESP, RESP), RESP)

    def arrive(r):
        for kind in (0, 1):
            await_recv((q_st, do_st)[kind].at[qrows(r)], xr.at[kind, r])

    def query_grad(o, ds_old):
        dqh = (nn(k_t[o // RATIO], ds_old[...]) * SCALE).T
        dq_out[:, pl.ds(pl.multiple_of(o * D, D), D)] = dqh.astype(BF16)
        b_z[zpos, pl.ds(o, 1)] = jnp.sum(dqh, axis=0, keepdims=True)

    def step(r, p_new, ds_new, p_old, ds_old):
        arrive(r)
        kv = r // RATIO
        qh = q_st[qrows(r)]
        ch = (do_st[qrows(r)].astype(F32) * factor).astype(BF16)
        c_st[qrows(r)] = ch
        o = r - 1
        top = total = accum = None
        if p_old is not None:
            okv = o // RATIO
            qo = q_st[qrows(o)]
            co = c_st[qrows(o)]

        for b in range(nblk):
            s = nt(kv_all[kv, blk(b), :D], qh)
            if b == nblk - 1:
                s = jnp.where(seen(), s, -1e30)
            s_buf[blk(b)] = s
            m = fold(s, jnp.max)
            top = m if top is None else jnp.maximum(top, m)
        top = jnp.max(top, axis=0, keepdims=True) * C2
        if p_old is not None:
            query_grad(o, ds_old)
        for b in range(nblk):
            if p_old is not None:
                acc_kv[okv, blk(b), D:] += nn(p_old[blk(b)], co)
            dpr = nt(kv_all[kv, blk(b), D:], ch)
            e = jnp.exp2(s_buf[blk(b)] * C2 - top)
            s_buf[blk(b)] = e
            dp_buf[blk(b)] = dpr
            t1 = fold(e, jnp.sum)
            t2 = fold(e * dpr, jnp.sum)
            total = t1 if total is None else total + t1
            accum = t2 if accum is None else accum + t2
        total = jnp.sum(total, axis=0, keepdims=True)
        accum = jnp.sum(accum, axis=0, keepdims=True)
        inv = 1.0 / total
        delta = accum * inv
        for b in range(nblk):
            if p_old is not None:
                acc_kv[okv, blk(b), :D] += nn(ds_old[blk(b)], qo)
            p = s_buf[blk(b)] * inv
            p_new[blk(b)] = p.astype(BF16)
            ds_new[blk(b)] = (p * (dp_buf[blk(b)] - delta)).astype(BF16)

    far = (2, 1, 3, 0)

    def zrows(e):
        return pl.ds(pl.multiple_of(lax.rem(zh + e, NZ) * YROWS, YROWS), YROWS)

    def rsib(kv, e):
        rows = zrows(e)
        return remote(rs_snd.at[kv, rows], rs_sib.at[kv, rows], r0s.at[kv], r0r.at[kv, e], sib)

    def send_sib(kv):
        for e in far:
            rsib(kv, e).start()

    owners = [(e, d) for e in far for d in far if (e, d) != (0, 0)]

    def odev(e, d):
        return {"group": lax.rem(y + d, NY) * (2 * NZ) + lax.rem(zh + e, NZ) * 2 + core}

    def zyrows(e, d):
        zz, yy = lax.rem(zh + e, NZ), lax.rem(y + d, NY)
        return pl.ds(pl.multiple_of(zz * YROWS + yy * PIECE, PIECE), PIECE)

    lane = lax.broadcasted_iota(jnp.int32, (1, 2 * D), 1)
    scales = jnp.where(lane < D, SCALE, 1.0)

    def half(kv, c, rows=None):
        base = pl.multiple_of(c * HALF, HALF)
        rows = pl.ds(base, HALF) if rows is None else pl.ds(base + rows.start, rows.size)
        return acc_kv[kv, rows] * scales

    def own_rows(kv, rows):
        return half(kv, core, rows) + rs_sib[kv, rows].astype(F32)

    def reduce_send(kv):
        for group in ((2,), (1, 3, 0)):
            for e in group:
                rsib(kv, e).wait_recv()
                rs_snd2[kv, zrows(e)] = own_rows(kv, zrows(e)).astype(BF16)
            for d in far:
                for e in group:
                    if (e, d) != (0, 0):
                        src = rs_snd2.at[kv, zyrows(e, d)]
                        i = owners.index((e, d))
                        remote(src, rs_y.at[kv, i], r1s.at[kv], r1r.at[kv], odev(e, d)).start()

    def reduce_done(kv):
        await_recv(rs_y.at[kv], r1r.at[kv])
        acc = own_rows(kv, zyrows(0, 0))
        for i in range(len(owners)):
            acc = acc + rs_y[kv, i].astype(F32)
        dpk_out[:, kv * D : (kv + 1) * D] = acc[:, :D].astype(BF16)
        dpv_out[:, kv * D : (kv + 1) * D] = acc[:, D:].astype(BF16)

    nb = KV * RATIO

    def send_half(kv):
        rs_snd[kv] = half(kv, 1 - core).astype(BF16)
        send_sib(kv)

    def suffix(kv):
        lanes = slice(kv * D, (kv + 1) * D)
        dks = acc_kv[kv, PRE:, :D] * SCALE
        dvs = acc_kv[kv, PRE:, D:]
        dks_out[:, lanes] = dks.astype(BF16)
        dvs_out[:, lanes] = dvs.astype(BF16)
        b_z[zpos, nb + kv : nb + kv + 1] = jnp.sum(dks, axis=0, keepdims=True)
        b_z[zpos, nb + KV + kv : nb + KV + kv + 1] = jnp.sum(dvs, axis=0, keepdims=True)

    b_z[zpos] = jnp.zeros((16, D), F32)

    def ready(kv):
        gather_done(kv)
        await_recv(kv_all.at[kv, PRE:KEYS], kvr.at[kv])
        k_t[kv] = kv_all[kv, :, :D].T

    bufs_a, bufs_b = (p_a, ds_a), (p_b, ds_b)
    ready(0)
    step(0, *bufs_a, None, None)

    def pair(i, carry):
        @pl.when(i == 0)
        def _():
            for e in (0,) + order:
                gather_sib(1, e)

        @pl.when(i == 2)
        def _():
            ready(1)

        @pl.when(i == 3)
        def _():
            reduce_send(0)

        step(2 * i + 1, *bufs_b, *bufs_a)

        @pl.when(i == 2)
        def _():
            send_half(0)
            suffix(0)

        step(2 * i + 2, *bufs_a, *bufs_b)
        return carry

    lax.fori_loop(0, nb // 2 - 1, pair, 0)
    step(nb - 1, *bufs_b, *bufs_a)

    o = nb - 1
    qo = q_st[o * RESP : (o + 1) * RESP]
    co = c_st[o * RESP : (o + 1) * RESP]
    other = pl.ds(pl.multiple_of((1 - core) * HALF, HALF), HALF)
    mine = pl.ds(pl.multiple_of(core * HALF, HALF), HALF)
    rs_snd[1, :, :D] = ((acc_kv[1, other, :D] + nn(ds_b[other], qo)) * SCALE).astype(BF16)
    rs_snd[1, :, D:] = (acc_kv[1, other, D:] + nn(p_b[other], co)).astype(BF16)
    send_sib(1)
    for rows in (mine, slice(PRE, KEYS)):
        acc_kv[1, rows, :D] += nn(ds_b[rows], qo)
        acc_kv[1, rows, D:] += nn(p_b[rows], co)
    query_grad(o, ds_b)
    suffix(1)

    for d in (4, 3, 5, 2, 6, 1, 7):
        remote(b_z.at[zpos], b_z.at[zpos], bs2, br2, zzdev(d)).start()
    reduce_send(1)
    reduce_done(0)
    await_recv(b_z.at[0 : 2 * NZ - 1], br2)
    acc = b_z[0]
    for i in range(1, 2 * NZ):
        acc = acc + b_z[i]
    b_y[pl.ds(ypos, 1)] = acc[None]
    for d in (4, 3, 5, 2, 6, 1, 7):
        remote(b_y.at[ypos], b_y.at[ypos], bs1, br1, yydev(d)).start()

    for kind in (0, 1):
        await_send(q_st.at[0 : KV * RATIO * (NX - 1) * TOK], xs.at[kind])
    await_send(q_st.at[0 : 2 * KV * (NX - 1) * TOK], kvs)
    for kv in range(KV):
        await_send(kv_all.at[kv, 0 : (NZ - 1) * PIECE], gzs.at[kv])
        await_send(kv_all.at[kv, 0 : NZ * (NY - 1) * PIECE], gys.at[kv])
        await_send(kv_all.at[kv, 0:HALF], gss.at[kv])
        await_send(rs_snd.at[kv], r0s.at[kv])

    reduce_done(1)
    await_recv(b_y.at[0 : 2 * NY - 1], br1)
    acc = b_y[0]
    for i in range(1, 2 * NY):
        acc = acc + b_y[i]
    qb_out[...] = acc[:nb]
    for kv in range(KV):
        kvb_out[0:1, kv * D : (kv + 1) * D] = acc[nb + kv : nb + kv + 1]
        kvb_out[1:2, kv * D : (kv + 1) * D] = acc[nb + KV + kv : nb + KV + kv + 1]
    for kv in range(KV):
        await_send(rs_y.at[kv], r1s.at[kv])
    await_send(b_z.at[0 : 2 * NZ - 1], bs2)
    await_send(b_y.at[0 : 2 * NY - 1], bs1)


def finish(*refs):
    n = (len(refs) - 1) // 2
    sem = refs[-1]
    copies = []
    for i in range(n):
        src, dst = refs[i], refs[n + i]
        parts = 4 if i == 0 else 1
        rows = src.shape[0] // parts
        for j in range(parts):
            part = pl.ds(j * rows, rows)
            copies.append(pltpu.make_async_copy(src.at[part], dst.at[part], sem.at[len(copies)]))
    for copy in copies:
        copy.start()
    for copy in copies:
        copy.wait()


def local(queries, suffix_keys, suffix_values, d_out, prefix_keys, prefix_values, advantages, lengths):
    sds = jax.ShapeDtypeStruct
    dma = pltpu.SemaphoreType.DMA
    hbm = pl.BlockSpec(memory_space=pl.ANY)
    smem = pl.BlockSpec(memory_space=pltpu.SMEM)
    nb = KV * RATIO
    vm = pltpu.VMEM
    shapes = (
        sds((RESP, KV * QC), BF16),
        sds((RESP, KV * D), BF16),
        sds((RESP, KV * D), BF16),
        sds((PIECE, KV * D), BF16),
        sds((PIECE, KV * D), BF16),
        sds((nb, D), F32),
        sds((2, KV * D), F32),
    )
    out = pl.pallas_call(
        kernel,
        out_shape=tuple(vm(s.shape, s.dtype) for s in shapes),
        in_specs=[hbm] * 6 + [smem] * 2,
        out_specs=(pl.BlockSpec(memory_space=vm),) * 7,
        scratch_shapes=[
            vm((KV * QT, D), BF16), vm((KV * QT, D), BF16), vm((KV * QT, D), BF16),
            vm((KV, KEYS, 2 * D), BF16),
            vm((KV, D, KEYS), BF16),
            vm((KEYS, RESP), F32), vm((KEYS, RESP), F32),
            vm((KEYS, RESP), BF16), vm((KEYS, RESP), BF16), vm((KEYS, RESP), BF16), vm((KEYS, RESP), BF16),
            vm((KV, KEYS, 2 * D), F32),
            vm((KV, HALF, 2 * D), BF16), vm((KV, HALF, 2 * D), BF16),
            vm((KV, HALF, 2 * D), BF16), vm((KV, NY * NZ - 1, PIECE, 2 * D), BF16),
            vm((2 * NY, 16, D), F32), vm((2 * NZ, 16, D), F32),
            dma((2,)), dma((2, nb)), dma, dma((KV,)), dma((KV,)),
            dma((KV,)), dma((KV, NZ - 1)), dma((KV,)), dma((KV, NZ)), dma((KV,)), dma((KV,)),
            dma((KV,)), dma((KV, NZ)), dma((KV,)), dma((KV,)),
            dma, dma, dma, dma, dma,
        ],
        compiler_params=pltpu.CompilerParams(
            collective_id=0, has_side_effects=True, vmem_limit_bytes=60 * 1024 * 1024
        ),
        name="grouped_attention_backward",
    )(
        queries[0, 0], suffix_keys[0, 0], suffix_values[0, 0], d_out[0, 0],
        prefix_keys[0], prefix_values[0], advantages, lengths,
    )
    out = pl.pallas_call(
        finish,
        out_shape=shapes,
        in_specs=[hbm] * 7,
        out_specs=(hbm,) * 7,
        scratch_shapes=[dma((10,))],
        compiler_params=pltpu.CompilerParams(vmem_limit_bytes=4 * 1024 * 1024),
        name="finish",
    )(*out)
    dq, dks, dvs, dpk, dpv, qb, kvb = out
    return (dq[None, None], dks[None, None], dvs[None, None], dpk[None], dpv[None], qb.reshape(-1), kvb)


def solution(mesh):
    in_specs = (
        P("dp", "group", "tensor", None),
        P("dp", "group", "tensor", None),
        P("dp", "group", "tensor", None),
        P("dp", "group", "tensor", None),
        P("dp", "group", "tensor"),
        P("dp", "group", "tensor"),
        P("dp", "group"),
        P("dp", "group"),
    )
    out_specs = (
        P("dp", "group", None, "tensor"),
        P("dp", "group", None, "tensor"),
        P("dp", "group", None, "tensor"),
        P("dp", "group", "tensor"),
        P("dp", "group", "tensor"),
        P("tensor"),
        P(None, "tensor"),
    )
    return jax.shard_map(local, mesh=mesh, in_specs=in_specs, out_specs=out_specs, check_vma=False)
```
